128 devices in a mesh: rep: 2 (over x_lo), row: 16 (over z, x_hi, core), col: 4 (over y).
Axes of the slice: x: 4 (x_hi: 2, x_lo: 2; x = x_hi * 2 + x_lo), y: 4, z: 4, core: 2. Of those that a mesh axis runs over, the one named last changes fastest.
Arguments:
- tokens: bfloat16 [1024, 8192], P(('rep', 'row'), 'col'), may hold values from -6 to 6
- probe_bits: int32 [1024, 8192], P('rep', 'col'), may hold values from 0 to 1
- cot_codes: int32 [1024, 8192], P('rep', 'col'), may hold values from 40 to 207, as said below
- cot_scales: int32 [1024, 256], P('rep', 'col'), may hold values from -2 to 2
- w_gate: bfloat16 [8192, 14336], P('col', 'row'), may hold values from -0.0625 to 0.0625
- w_up: bfloat16 [8192, 14336], P('col', 'row'), may hold values from -0.0625 to 0.0625
- w_down: bfloat16 [14336, 8192], P('row', 'col'), may hold values from -0.046875 to 0.046875
Outputs:
- grad_out: bfloat16 [1024, 8192], P(('rep', 'row'), 'col')
- hess_out: bfloat16 [1024, 8192], P(('rep', 'row'), 'col')
- diag_out: float32 [8192], P('col')
The draws below stay inside these ranges and needn't reach their ends.
Inputs may be any that keep to these rules, and one draw needn't show every extreme that they name: `cot_codes`: each code is an E4M3 byte: sign in bit 7, exponent field (bits 3 to 6) from 5 to 9, mantissa in bits 0 to 2.
All inputs are finite; a program needn't handle non-finite values.
Results may differ from the reference program's by a relative error of at most 0.019.
Values may be sent and summed in bfloat16 or wider, within the bound.
A program may use at most 128 MiB of HBM per device.

```python
import jax
import jax.numpy as jnp

D = 8192
FF = 14336
TOKENS = 1024


def draw_cot_codes(key, part):
    key = jax.random.fold_in(key, 11)
    key_sign, key_field, key_mant = jax.random.split(key, 3)
    sign_bit = jax.random.randint(key_sign, (TOKENS, D), 0, 2)
    exponent = jax.random.randint(key_field, (TOKENS, D), 5, 10)
    mantissa = jax.random.randint(key_mant, (TOKENS, D), 0, 8)
    code_vals = sign_bit * 128 + exponent * 8 + mantissa
    code_vals = code_vals.at[0, 0].set(207).at[0, 1].set(40)
    return code_vals.astype(jnp.int32)


def touch_ends(entries, own_key, low, high):
    longest = entries.shape.index(max(entries.shape))
    spots = []
    for shift in (0, 1):
        where = [jax.random.randint(jax.random.fold_in(own_key, axis), (), 0, length) for axis, length in enumerate(entries.shape)]
        where[longest] = (where[longest] + shift) % entries.shape[longest]
        spots.append(tuple(where))
    return entries.at[spots[0]].set(low).at[spots[1]].set(high)


def level_of(own_key, extent, cuts, smallest, top_value):
    def one(position, parts):
        heights = jax.random.uniform(jax.random.fold_in(jax.random.fold_in(own_key, 6), position), (parts,), jnp.float32, smallest / len(cuts), top_value / len(cuts))
        return jnp.repeat(jnp.exp(heights), extent[position] // parts).reshape((-1,) + (1,) * (len(extent) - position - 1))

    gain = one(*cuts[0])
    for cut in cuts[1:]:
        gain = gain * one(*cut)
    return gain


def centred(stream_key, dims, width, bound, pieces=(), held_as=jnp.bfloat16):
    drawn = jax.random.normal(stream_key, dims, jnp.float32) * width
    if len(pieces) > 0:
        drawn = level_of(stream_key, dims, pieces, -0.22, 0.18) * drawn
    return jnp.clip(drawn, min=-bound, max=bound).astype(held_as)


def setup_inputs(seed: int = 0) -> dict:
    key_list = jax.random.split(jax.random.key(seed), 8)
    tokens = centred(key_list[0], (TOKENS, D), 1.0, 6.0, ((0, 32), (1, 4)))
    probe_bits = touch_ends(jax.random.randint(key_list[1], (TOKENS, D), 0, 2), jax.random.fold_in(key_list[1], 1), 0, 1).astype(jnp.int32)
    cot_codes = draw_cot_codes(jax.random.fold_in(key_list[7], 71), 0)
    cot_scales = touch_ends(jax.random.randint(key_list[3], (TOKENS, D // 32), -2, 3), jax.random.fold_in(key_list[3], 1), -2, 2).astype(jnp.int32)
    w_gate = centred(key_list[4], (D, FF), D ** -0.5, 0.0625, ((0, 4), (1, 16)))
    w_up = centred(key_list[5], (D, FF), D ** -0.5, 0.0625, ((0, 4), (1, 16)))
    w_down = centred(key_list[6], (FF, D), FF ** -0.5, 0.046875, ((0, 16), (1, 4)))
    return {"tokens": tokens, "probe_bits": probe_bits, "cot_codes": cot_codes, "cot_scales": cot_scales, "w_gate": w_gate, "w_up": w_up, "w_down": w_down}


def power_two(exponent):
    result = jnp.zeros(exponent.shape, jnp.float32)
    for level in range(-4, 5):
        result = jnp.where(exponent == level, jnp.float32(2.0 ** level), result)
    return result


def decode(code_vals, scale_exp):
    sign_val = (1 - 2 * (code_vals // 128)).astype(jnp.float32)
    field = (code_vals // 8) % 16
    mantissa = (code_vals % 8).astype(jnp.float32)
    expanded = jnp.repeat(scale_exp, 32, axis=1)
    return sign_val * (1.0 + mantissa / 8.0) * power_two(field - 7 + expanded)


def local_terms(gate_pre, up_pre, gate_tan, up_tan, down_back):
    sig_gate = jax.nn.sigmoid(gate_pre)
    first_der = sig_gate * (1.0 + gate_pre * (1.0 - sig_gate))
    second_der = sig_gate * (1.0 - sig_gate) * (2.0 + gate_pre * (1.0 - 2.0 * sig_gate))
    term_a = (down_back * up_pre * first_der).astype(jnp.bfloat16)
    term_b = (down_back * gate_pre * sig_gate).astype(jnp.bfloat16)
    term_c = (down_back * (up_tan * first_der + up_pre * second_der * gate_tan)).astype(jnp.bfloat16)
    term_d = (down_back * first_der * gate_tan).astype(jnp.bfloat16)
    return term_a, term_b, term_c, term_d


def reference(tokens, probe_bits, cot_codes, cot_scales, w_gate, w_up, w_down):
    signs = (2 * probe_bits - 1).astype(jnp.bfloat16)
    cotangent = decode(cot_codes, cot_scales).astype(jnp.bfloat16)
    gate_pre = jnp.dot(tokens, w_gate, preferred_element_type=jnp.float32)
    up_pre = jnp.dot(tokens, w_up, preferred_element_type=jnp.float32)
    gate_tan = jnp.dot(signs, w_gate, preferred_element_type=jnp.float32)
    up_tan = jnp.dot(signs, w_up, preferred_element_type=jnp.float32)
    down_back = jnp.dot(cotangent, w_down.T, preferred_element_type=jnp.float32)
    term_a, term_b, term_c, term_d = local_terms(gate_pre, up_pre, gate_tan, up_tan, down_back)
    grad_full = jnp.dot(term_a, w_gate.T, preferred_element_type=jnp.float32) + jnp.dot(term_b, w_up.T, preferred_element_type=jnp.float32)
    hess_full = jnp.dot(term_c, w_gate.T, preferred_element_type=jnp.float32) + jnp.dot(term_d, w_up.T, preferred_element_type=jnp.float32)
    diag_out = jnp.sum(signs.astype(jnp.float32) * hess_full, axis=0) / jnp.float32(TOKENS)
    return grad_full.astype(jnp.bfloat16), hess_full.astype(jnp.bfloat16), diag_out
```

```python
import functools

import jax
import jax.numpy as jnp
from jax import lax
from jax.experimental import pallas as pl
from jax.experimental.pallas import tpu as pltpu
from jax.sharding import PartitionSpec as P

MESH = pl.DeviceIdType.MESH
BF = jnp.bfloat16
F32 = jnp.float32
REPS, ROWS, COLS = 2, 16, 4
CHIPS = ROWS // 2
NCH = 4
SUB = 8
CT = ROWS * SUB
OWN = CT // COLS
HALF = OWN // 2
FE = 2048
HI = 896
HI2, HI3 = 2 * HI, 3 * HI
NT = (((1,), (1,)), ((), ()))


def aligned(value, step):
    return pl.multiple_of(value, step)


def kernel(
    tok, bits_hbm, codes_hbm, scales_hbm, wg_hbm, wu_hbm, wd_hbm,
    grad_out, hess_out, diag_out,
    w, wd, bits, codes, scales, spread, signs, cot, gathered, ordered,
    part1, part2, in1, in2, red1, red2, terms, total, mine,
    pair_out, pair_in, row_out, row_in, dsum, dbuf1, dbuf2, res,
    load_sem, tok_send, tok_recv, sib_send, sib_recv,
    rs1_send, rs1_recv, rs2_send, rs2_recv, ag1_send, ag1_recv, ag2_send, ag2_recv,
    pair_send, pair_recv, row_send, row_recv, d1_send, d1_recv, d2_send, d2_recv,
):
    rep = lax.axis_index("rep")
    row = lax.axis_index("row")
    col = lax.axis_index("col")
    core = lax.rem(row, 2)
    chip = row // 2
    sib = row + 1 - 2 * core
    left = lax.rem(col + COLS - 1, COLS)
    right = lax.rem(col + 1, COLS)
    opp = lax.rem(col + 2, COLS)
    sides = (left, right)

    def peer(step):
        other = lax.rem(chip + step, CHIPS)
        return other, 2 * other + core

    def load_bits(k):
        return pltpu.make_async_copy(bits_hbm.at[:, k], bits.at[k], load_sem.at[k])

    def load_codes(k):
        return pltpu.make_async_copy(codes_hbm.at[:, k], codes.at[k], load_sem.at[NCH + k])

    load_wg = pltpu.make_async_copy(wg_hbm, w.at[:, pl.ds(0, HI)], load_sem.at[2 * NCH])
    load_wu = pltpu.make_async_copy(wu_hbm, w.at[:, pl.ds(HI, HI)], load_sem.at[2 * NCH + 1])
    load_wd = pltpu.make_async_copy(wd_hbm, wd, load_sem.at[2 * NCH + 2])
    load_sc = pltpu.make_async_copy(scales_hbm, scales, load_sem.at[2 * NCH + 3])
    load_bits(0).start()
    load_wg.start()
    load_wu.start()
    load_codes(0).start()
    load_sc.start()
    load_wd.start()
    for k in range(1, NCH):
        load_bits(k).start()
        load_codes(k).start()

    barrier = pltpu.get_barrier_semaphore()
    for side in sides:
        pl.semaphore_signal(barrier, inc=1, device_id={"col": side}, device_id_type=MESH)
    pl.semaphore_signal(barrier, inc=1, device_id={"row": sib}, device_id_type=MESH)
    for other_row in (row, sib):
        pl.semaphore_signal(
            barrier, inc=1, device_id={"rep": 1 - rep, "row": other_row}, device_id_type=MESH
        )
    for step in range(1, CHIPS):
        pl.semaphore_signal(barrier, inc=1, device_id={"row": peer(step)[1]}, device_id_type=MESH)
    pl.semaphore_wait(barrier, 5 + CHIPS - 1)

    def remote(src, dst, send, recv, where):
        return pltpu.make_async_remote_copy(
            src_ref=src, dst_ref=dst, send_sem=send, recv_sem=recv, device_id=where, device_id_type=MESH
        )

    def send_tok(step):
        other, where = peer(step)
        return remote(tok, gathered.at[row], tok_send.at[other], tok_recv.at[chip], {"row": where})

    def recv_tok(other):
        block = gathered.at[2 * other + core]
        return remote(block, block, tok_send.at[other], tok_recv.at[other], {"row": sib})

    def own_to_sib():
        return remote(tok, gathered.at[row], sib_send.at[chip], sib_recv.at[chip], {"row": sib})

    def relay(other):
        block = gathered.at[2 * other + core]
        return remote(block, block, sib_send.at[other], sib_recv.at[other], {"row": sib})

    own_to_sib().start()
    for step in range(1, CHIPS):
        send_tok(step).start()
    gathered[row] = tok[...]

    lanes = lax.broadcasted_iota(jnp.int32, spread.shape, 1) // 32
    spread[...] = (lanes == lax.broadcasted_iota(jnp.int32, spread.shape, 0)).astype(F32).astype(BF)

    def rs1(batch, k, side):
        part, inn = ((part1, in1), (part2, in2))[batch]
        src = part.at[k, pl.ds(aligned(OWN * opp + HALF * side, HALF), HALF)]
        at = NCH * batch + k
        return remote(
            src, inn.at[side, k], rs1_send.at[side, at], rs1_recv.at[side, at], {"col": sides[side]}
        )

    def rs2(batch, k, side):
        part, red = ((part1, red1), (part2, red2))[batch]
        src = part.at[k, pl.ds(aligned(OWN * sides[side], OWN), OWN)]
        at = NCH * batch + k
        return remote(
            src, red.at[side, k], rs2_send.at[side, at], rs2_recv.at[side, at], {"col": sides[side]}
        )

    def fold(batch, k):
        part, inn = ((part1, in1), (part2, in2))[batch]
        for side in range(2):
            rs1(batch, k, side).wait_recv()
            rows = pl.ds(aligned(OWN * sides[side] + HALF * side, HALF), HALF)
            part[k, rows] = (part[k, rows].astype(F32) + inn[side, k].astype(F32)).astype(BF)
            rs2(batch, k, side).start()

    def forward1(k):
        load_bits(k).wait()
        signs[k] = (2 * bits[k].reshape(CT, FE) - 1).astype(F32).astype(BF)

        @pl.when(k == 0)
        def _():
            load_wg.wait()
            load_wu.wait()

        @pl.loop(0, HI2 // 256)
        def _(n):
            cols = pl.ds(aligned(n * 256, 256), 256)
            part1[k, :, cols] = jnp.dot(signs[k], w[:, cols], preferred_element_type=F32).astype(BF)

        load_codes(k).wait()

        @pl.when(k == 0)
        def _():
            load_sc.wait()
            load_wd.wait()

        power = (lax.shift_left(1, scales[:, k].reshape(CT, FE // 32) + 2).astype(F32) * 2.0**-7).astype(BF)

        @pl.loop(0, FE // 512)
        def _(n):
            cols = pl.ds(aligned(n * 512, 512), 512)
            code = codes[k, :, :, cols].reshape(CT, 512)
            size = lax.shift_left((code & 7) | 8, ((code >> 3) & 15) - 5)
            value = jnp.where(code >= 128, -size, size).astype(F32)
            wide = jnp.dot(power, spread[:, cols], preferred_element_type=F32)
            cot[:, cols] = (value * wide).astype(BF)

        for start in range(0, HI, 256):
            wide = min(256, HI - start)
            part1[k, :, pl.ds(HI2 + start, wide)] = lax.dot_general(
                cot[...], wd[pl.ds(start, wide), :], NT, preferred_element_type=F32
            ).astype(BF)
        for side in range(2):
            rs1(0, k, side).start()

    def forward2(k):
        @pl.loop(0, HI2 // 256)
        def _(n):
            cols = pl.ds(aligned(n * 256, 256), 256)
            part2[k, :, cols] = jnp.dot(ordered[k], w[:, cols], preferred_element_type=F32).astype(BF)

        for side in range(2):
            rs1(1, k, side).start()

    def gather_tokens():
        @pl.loop(1, CHIPS)
        def _(step):
            other = peer(step)[0]
            recv_tok(other).wait_recv()
            relay(other).start()

        @pl.loop(0, CHIPS)
        def _(other):
            relay(other).wait_recv()

        @pl.loop(0, CHIPS)
        def _(q):
            for h in range(NCH // 2):
                rows = pl.ds(2 * SUB * h, 2 * SUB)
                even = gathered[2 * q, rows].astype(F32)
                odd = gathered[2 * q + 1, rows].astype(F32)
                out = pl.ds(aligned(2 * SUB * q, 2 * SUB), 2 * SUB)
                ordered[2 * h, out] = jnp.concatenate([even[:SUB], odd[:SUB]], axis=0).astype(BF)
                ordered[2 * h + 1, out] = jnp.concatenate([even[SUB:], odd[SUB:]], axis=0).astype(BF)

    @pl.loop(0, 2 * NCH + 1)
    def _(s):
        @pl.when(s < NCH)
        def _():
            forward1(s)

        @pl.when(s == NCH)
        def _():
            gather_tokens()

        @pl.when(jnp.logical_and(s >= NCH, s < 2 * NCH))
        def _():
            forward2(s - NCH)

        @pl.when(jnp.logical_and(s >= 1, s <= NCH))
        def _():
            fold(0, s - 1)

        @pl.when(s > NCH)
        def _():
            fold(1, s - 1 - NCH)

    def ag1(k, side):
        block = terms.at[k, :, pl.ds(aligned(OWN * col, OWN), OWN)]
        return remote(block, block, ag1_send.at[side, k], ag1_recv.at[side, k], {"col": sides[side]})

    def ag2(k, side):
        rows = pl.ds(aligned(OWN * sides[1 - side] + HALF * side, HALF), HALF)
        block = terms.at[k, :, rows]
        return remote(block, block, ag2_send.at[side, k], ag2_recv.at[side, k], {"col": sides[side]})

    def work_terms(k):
        for batch in range(2):
            for side in range(2):
                rs2(batch, k, side).wait_recv()
        rows = pl.ds(aligned(OWN * col, OWN), OWN)

        def full(part, red, start):
            cols = pl.ds(start, 128)
            return part[k, rows, cols].astype(F32) + red[0, k, :, cols].astype(F32) + red[1, k, :, cols].astype(F32)

        for start in range(0, HI, 128):
            gate_tan = full(part1, red1, start)
            up_tan = full(part1, red1, HI + start)
            down_back = full(part1, red1, HI2 + start)
            gate_pre = full(part2, red2, start)
            up_pre = full(part2, red2, HI + start)
            sig = 1.0 / (1.0 + jnp.exp(-gate_pre))
            rest = 1.0 - sig
            first = sig * (1.0 + gate_pre * rest)
            second = sig * rest * (2.0 + gate_pre * (1.0 - 2.0 * sig))
            down_first = down_back * first
            terms[k, 0, rows, pl.ds(start, 128)] = (down_first * up_pre).astype(BF)
            terms[k, 0, rows, pl.ds(HI + start, 128)] = (down_back * gate_pre * sig).astype(BF)
            terms[k, 1, rows, pl.ds(start, 128)] = (
                down_back * (up_tan * first + up_pre * second * gate_tan)
            ).astype(BF)
            terms[k, 1, rows, pl.ds(HI + start, 128)] = (down_first * gate_tan).astype(BF)
        for side in range(2):
            ag1(k, side).start()

    def forward_terms(k):
        for side in range(2):
            ag1(k, side).wait_recv()
            ag2(k, side).start()

    def pair(k):
        return remote(pair_out.at[k], pair_in.at[k], pair_send.at[k], pair_recv.at[k], {"row": sib})

    def row_copy(k, step):
        other, where = peer(step)
        return remote(
            row_out.at[k, other], row_in.at[k, chip], row_send.at[k, other], row_recv.at[k, chip], {"row": where}
        )

    def row_wait(k, other):
        return remote(
            row_out.at[k, other], row_in.at[k, other], row_send.at[k, other], row_recv.at[k, other], {"row": sib}
        )

    dsum[...] = jnp.zeros_like(dsum)

    def backward(k):
        for side in range(2):
            ag2(k, side).wait_recv()

        @pl.loop(0, FE // 512)
        def _(n):
            cols = pl.ds(aligned(n * 512, 512), 512)
            out = lax.dot_general(
                terms[k].reshape(2 * CT, HI2), w[cols, :], NT, preferred_element_type=F32
            )
            res[:, cols] = out
            prod = out[CT:] * signs[k, :, cols].astype(F32)
            dsum[:, cols] += jnp.sum(prod.reshape(CT // 8, 8, 512), axis=0)

        slot = lax.rem(k, 2)

        @pl.loop(0, CHIPS)
        def _(m):
            rows = pl.ds(aligned(2 * SUB * m, 2 * SUB), 2 * SUB)
            for keep, at in ((False, 1 - core), (True, core)):
                first = aligned(2 * SUB * m + SUB * at, SUB)
                both = jnp.concatenate(
                    [res[pl.ds(first, SUB), :], res[pl.ds(aligned(CT + first, SUB), SUB), :]], axis=0
                )
                if keep:
                    mine[slot, rows] = both
                else:
                    pair_out[k, rows] = both.astype(BF)

        pair(k).start()

    def send_rows(k):
        pair(k).wait_recv()
        slot = lax.rem(k, 2)

        @pl.loop(0, CHIPS)
        def _(m):
            rows = pl.ds(aligned(2 * SUB * m, 2 * SUB), 2 * SUB)
            row_out[k, m] = (mine[slot, rows] + pair_in[k, rows].astype(F32)).astype(BF)

        @pl.loop(1, CHIPS)
        def _(step):
            row_copy(k, step).start()

        row_in[k, chip] = row_out[k, chip]

    def finish(k):
        @pl.loop(1, CHIPS)
        def _(step):
            row_wait(k, peer(step)[0]).wait_recv()

        total_k = row_in[k, 0].astype(F32)
        for m in range(1, CHIPS):
            total_k = total_k + row_in[k, m].astype(F32)
        total[0, pl.ds(aligned(SUB * k, SUB), SUB)] = total_k[:SUB]
        total[1, pl.ds(aligned(SUB * k, SUB), SUB)] = total_k[SUB:]

    def d1(step):
        other, where = peer(step)
        return remote(dbuf1.at[chip], dbuf1.at[chip], d1_send.at[other], d1_recv.at[chip], {"row": where})

    def d1_wait(other):
        return remote(dbuf1.at[other], dbuf1.at[other], d1_send.at[other], d1_recv.at[other], {"row": sib})

    quad = 2 * rep + core

    def d2(which):
        where = ({"row": sib}, {"rep": 1 - rep}, {"rep": 1 - rep, "row": sib})[which]
        return remote(dbuf2.at[quad], dbuf2.at[quad], d2_send.at[which], d2_recv.at[which], where)

    @pl.loop(0, NCH + 4)
    def _(s):
        @pl.when(s < NCH)
        def _():
            work_terms(s)

        @pl.when(jnp.logical_and(s >= 1, s < NCH + 1))
        def _():
            forward_terms(s - 1)

        @pl.when(jnp.logical_and(s >= 3, s < NCH + 3))
        def _():
            send_rows(s - 3)

        @pl.when(jnp.logical_and(s >= 2, s < NCH + 2))
        def _():
            backward(s - 2)

        @pl.when(s == NCH + 1)
        def _():
            dbuf1[chip] = jnp.sum(dsum[...], axis=0, keepdims=True)
            for step in range(1, CHIPS):
                d1(step).start()

        @pl.when(s == NCH + 2)
        def _():
            for step in range(1, CHIPS):
                d1_wait(peer(step)[0]).wait_recv()
            dbuf2[quad] = jnp.sum(dbuf1[...], axis=0)
            for which in range(3):
                d2(which).start()

        @pl.when(s >= 4)
        def _():
            finish(s - 4)

    grad_out[...] = total[0].astype(BF)
    hess_out[...] = total[1].astype(BF)
    for which in range(3):
        d2(which).wait_recv()
    diag_out[...] = jnp.sum(dbuf2[...], axis=0) * (1.0 / (REPS * ROWS * NCH * SUB))

    own_to_sib().wait_send()
    for which in range(3):
        d2(which).wait_send()

    @pl.loop(1, CHIPS)
    def _(step):
        send_tok(step).wait_send()
        relay(peer(step)[0]).wait_send()
        d1(step).wait_send()

    @pl.loop(0, NCH)
    def _(k):
        for side in range(2):
            for batch in range(2):
                rs1(batch, k, side).wait_send()
                rs2(batch, k, side).wait_send()
            ag1(k, side).wait_send()
            ag2(k, side).wait_send()
        pair(k).wait_send()

        @pl.loop(1, CHIPS)
        def _(step):
            row_copy(k, step).wait_send()


def local(tokens, probe_bits, cot_codes, cot_scales, w_gate, w_up, w_down):
    split = (ROWS, NCH, SUB)
    vm = pl.BlockSpec(memory_space=pltpu.VMEM)
    hbm = pl.BlockSpec(memory_space=pl.ANY)
    dma = pltpu.SemaphoreType.DMA
    grad, hess, diag = pl.pallas_call(
        kernel,
        out_shape=(
            jax.ShapeDtypeStruct((NCH * SUB, FE), BF),
            jax.ShapeDtypeStruct((NCH * SUB, FE), BF),
            jax.ShapeDtypeStruct((1, FE), F32),
        ),
        in_specs=[vm] + [hbm] * 6,
        out_specs=[vm] * 3,
        scratch_shapes=[
            pltpu.VMEM((FE, HI2), BF),
            pltpu.VMEM((HI, FE), BF),
            pltpu.VMEM((NCH, ROWS, SUB, FE), jnp.int32),
            pltpu.VMEM((NCH, ROWS, SUB, FE), jnp.int32),
            pltpu.VMEM((ROWS, NCH, SUB, FE // 32), jnp.int32),
            pltpu.VMEM((FE // 32, FE), BF),
            pltpu.VMEM((NCH, CT, FE), BF),
            pltpu.VMEM((CT, FE), BF),
            pltpu.VMEM((ROWS, NCH * SUB, FE), BF),
            pltpu.VMEM((NCH, CT, FE), BF),
            pltpu.VMEM((NCH, CT, HI3), BF),
            pltpu.VMEM((NCH, CT, HI2), BF),
            pltpu.VMEM((2, NCH, HALF, HI3), BF),
            pltpu.VMEM((2, NCH, HALF, HI2), BF),
            pltpu.VMEM((2, NCH, OWN, HI3), BF),
            pltpu.VMEM((2, NCH, OWN, HI2), BF),
            pltpu.VMEM((NCH, 2, CT, HI2), BF),
            pltpu.VMEM((2, NCH * SUB, FE), F32),
            pltpu.VMEM((2, CT, FE), F32),
            pltpu.VMEM((NCH, CT, FE), BF),
            pltpu.VMEM((NCH, CT, FE), BF),
            pltpu.VMEM((NCH, CHIPS, 2 * SUB, FE), BF),
            pltpu.VMEM((NCH, CHIPS, 2 * SUB, FE), BF),
            pltpu.VMEM((8, FE), F32),
            pltpu.VMEM((CHIPS, 1, FE), F32),
            pltpu.VMEM((4, 1, FE), F32),
            pltpu.VMEM((2 * CT, FE), F32),
            dma((2 * NCH + 4,)),
            dma((CHIPS,)), dma((CHIPS,)), dma((CHIPS,)), dma((CHIPS,)),
            dma((2, 2 * NCH)), dma((2, 2 * NCH)), dma((2, 2 * NCH)), dma((2, 2 * NCH)),
            dma((2, NCH)), dma((2, NCH)), dma((2, NCH)), dma((2, NCH)),
            dma((NCH,)), dma((NCH,)),
            dma((NCH, CHIPS)), dma((NCH, CHIPS)),
            dma((CHIPS,)), dma((CHIPS,)), dma((3,)), dma((3,)),
        ],
        compiler_params=pltpu.CompilerParams(
            collective_id=0, has_side_effects=True, vmem_limit_bytes=63 * 2**20
        ),
    )(
        tokens,
        probe_bits.reshape(split + (FE,)),
        cot_codes.reshape(split + (FE,)),
        cot_scales.reshape(split + (FE // 32,)),
        w_gate,
        w_up,
        w_down,
    )
    return grad, hess, diag.reshape(FE)


def solution(mesh):
    in_specs = (
        P(("rep", "row"), "col"),
        P("rep", "col"),
        P("rep", "col"),
        P("rep", "col"),
        P("col", "row"),
        P("col", "row"),
        P("row", "col"),
    )
    out_specs = (P(("rep", "row"), "col"), P(("rep", "row"), "col"), P("col"))
    return jax.shard_map(local, mesh=mesh, in_specs=in_specs, out_specs=out_specs, check_vma=False)
```

```python
import functools

import jax
import jax.numpy as jnp
from jax import lax
from jax.experimental import pallas as pl
from jax.experimental.pallas import tpu as pltpu
from jax.sharding import PartitionSpec as P

MESH = pl.DeviceIdType.MESH
BF = jnp.bfloat16
F32 = jnp.float32
REPS, ROWS, COLS = 2, 16, 4
CHIPS = ROWS // 2
NCH = 4
SUB = 8
CT = ROWS * SUB
OWN = CT // COLS
HALF = OWN // 2
FE = 2048
HI = 896
HI2 = 2 * HI
FH = FE // 2
NT = (((1,), (1,)), ((), ()))


def aligned(value, step):
    return pl.multiple_of(value, step)


def kernel(
    tok, bits_hbm, codes_hbm, scales_hbm, wg_hbm, wu_hbm, wd_hbm,
    total, diag_out,
    w, wd, bits, codes, scales, spread, power, signs, cot, gathered, ordered,
    part0, part1, part2, in0, in1, in2, red0, red1, red2, terms, mine,
    pair_out, pair_in, row_out, row_in, dsum, dbuf1, dbuf2, res,
    load_sem, tok_send, tok_recv, sib_send, sib_recv,
    rs1_send, rs1_recv, rs2_send, rs2_recv, ag1_send, ag1_recv, ag2_send, ag2_recv,
    pair_send, pair_recv, row_send, row_recv, d1_send, d1_recv, d2_send, d2_recv,
):
    rep = lax.axis_index("rep")
    row = lax.axis_index("row")
    col = lax.axis_index("col")
    core = lax.rem(row, 2)
    chip = row // 2
    sib = row + 1 - 2 * core
    left = lax.rem(col + COLS - 1, COLS)
    right = lax.rem(col + 1, COLS)
    opp = lax.rem(col + 2, COLS)
    sides = (left, right)

    def peer(step):
        other = lax.rem(chip + step, CHIPS)
        return other, 2 * other + core

    def load_bits(k):
        return pltpu.make_async_copy(bits_hbm.at[:, k], bits.at[k], load_sem.at[k])

    def load_codes(k):
        return pltpu.make_async_copy(codes_hbm.at[:, k], codes.at[k], load_sem.at[NCH + k])

    load_wg = pltpu.make_async_copy(wg_hbm, w.at[:, pl.ds(0, HI)], load_sem.at[2 * NCH])
    load_wu = pltpu.make_async_copy(wu_hbm, w.at[:, pl.ds(HI, HI)], load_sem.at[2 * NCH + 1])
    load_wd = pltpu.make_async_copy(wd_hbm, wd, load_sem.at[2 * NCH + 2])
    load_sc = pltpu.make_async_copy(scales_hbm, scales, load_sem.at[2 * NCH + 3])
    load_sc.start()
    load_codes(0).start()
    load_codes(1).start()
    load_wd.start()
    load_codes(2).start()
    load_codes(3).start()
    load_bits(0).start()
    load_wg.start()
    load_wu.start()
    for k in range(1, NCH):
        load_bits(k).start()

    barrier = pltpu.get_barrier_semaphore()
    for side in sides:
        pl.semaphore_signal(barrier, inc=1, device_id={"col": side}, device_id_type=MESH)
    pl.semaphore_signal(barrier, inc=1, device_id={"row": sib}, device_id_type=MESH)
    for other_row in (row, sib):
        pl.semaphore_signal(
            barrier, inc=1, device_id={"rep": 1 - rep, "row": other_row}, device_id_type=MESH
        )
    for step in range(1, CHIPS):
        pl.semaphore_signal(barrier, inc=1, device_id={"row": peer(step)[1]}, device_id_type=MESH)
    pl.semaphore_wait(barrier, 5 + CHIPS - 1)

    def remote(src, dst, send, recv, where):
        return pltpu.make_async_remote_copy(
            src_ref=src, dst_ref=dst, send_sem=send, recv_sem=recv, device_id=where, device_id_type=MESH
        )

    def send_tok(step):
        other, where = peer(step)
        return remote(tok, gathered.at[row], tok_send.at[other], tok_recv.at[chip], {"row": where})

    def recv_tok(other):
        block = gathered.at[2 * other + core]
        return remote(block, block, tok_send.at[other], tok_recv.at[other], {"row": sib})

    def own_to_sib():
        return remote(tok, gathered.at[row], sib_send.at[chip], sib_recv.at[chip], {"row": sib})

    def relay(other):
        block = gathered.at[2 * other + core]
        return remote(block, block, sib_send.at[other], sib_recv.at[other], {"row": sib})

    own_to_sib().start()
    for step in range(1, CHIPS):
        send_tok(step).start()
    gathered[row] = tok[...]

    lanes = lax.broadcasted_iota(jnp.int32, spread.shape, 1) // 32
    spread[...] = (lanes == lax.broadcasted_iota(jnp.int32, spread.shape, 0)).astype(F32).astype(BF)
    at = lax.broadcasted_iota(jnp.int32, (NCH * CT, NCH * CT), 0)
    token = (at % CT) // SUB * (NCH * SUB) + at // CT * SUB + at % SUB
    pick = (token == lax.broadcasted_iota(jnp.int32, (NCH * CT, NCH * CT), 1)).astype(F32).astype(BF)
    load_sc.wait()
    raised = (lax.shift_left(1, scales[...] + 2).astype(F32) * 2.0**-7).astype(BF)
    power[...] = lax.dot_general(pick, raised, NT, preferred_element_type=F32).astype(BF)

    batches = ((part0, in0, red0, 2, 0), (part1, in1, red1, 1, 2), (part2, in2, red2, 1, 2 + NCH))

    def rs1(batch, k, side):
        part, inn, _, n, base = batches[batch]
        ks = pl.ds(k * n, n)
        src = part.at[ks, pl.ds(aligned(OWN * opp + HALF * side, HALF), HALF)]
        return remote(
            src, inn.at[side, ks], rs1_send.at[side, base + k], rs1_recv.at[side, base + k], {"col": sides[side]}
        )

    def rs2(batch, k, side):
        part, _, red, n, base = batches[batch]
        ks = pl.ds(k * n, n)
        src = part.at[ks, pl.ds(aligned(OWN * sides[side], OWN), OWN)]
        return remote(
            src, red.at[side, ks], rs2_send.at[side, base + k], rs2_recv.at[side, base + k], {"col": sides[side]}
        )

    def start_rs1(batch, k):
        for side in range(2):
            rs1(batch, k, side).start()

    def fold(batch, k):
        part, inn, _, n, _ = batches[batch]
        for side in range(2):
            rs1(batch, k, side).wait_recv()
            rows = pl.ds(aligned(OWN * sides[side] + HALF * side, HALF), HALF)
            for i in range(n):
                at = k * n + i
                part[at, rows] = (part[at, rows].astype(F32) + inn[side, at].astype(F32)).astype(BF)
            rs2(batch, k, side).start()

    def down(p):
        for i in range(2):
            load_codes(2 * p + i).wait()

        @pl.loop(0, FE // 512)
        def _(n):
            cols = pl.ds(aligned(n * 512, 512), 512)
            code = codes[pl.ds(2 * p, 2), :, :, cols].reshape(2 * CT, 512)
            size = lax.shift_left((code & 7) | 8, ((code >> 3) & 15) - 5)
            value = jnp.where(code >= 128, -size, size).astype(F32)
            wide = jnp.dot(
                power[pl.ds(aligned(2 * CT * p, 2 * CT), 2 * CT), :], spread[:, cols], preferred_element_type=F32
            )
            cot[:, cols] = (value * wide).astype(BF)

        @pl.when(p == 0)
        def _():
            load_wd.wait()

        part0[pl.ds(2 * p, 2)] = (
            lax.dot_general(cot[...], wd[...], NT, preferred_element_type=F32).astype(BF).reshape(2, CT, HI)
        )
        start_rs1(0, p)

    def tangent(k):
        load_bits(k).wait()
        signs[k] = (2 * bits[k].reshape(CT, FE) - 1).astype(F32).astype(BF)

        @pl.when(k == 0)
        def _():
            load_wg.wait()
            load_wu.wait()

        part1[k] = jnp.dot(signs[k], w[...], preferred_element_type=F32).astype(BF)
        start_rs1(1, k)

    def primal(k):
        part2[k] = jnp.dot(ordered[k], w[...], preferred_element_type=F32).astype(BF)
        start_rs1(2, k)

    def gather_tokens():
        @pl.loop(1, CHIPS)
        def _(step):
            other = peer(step)[0]
            recv_tok(other).wait_recv()
            relay(other).start()

    def order_tokens():
        @pl.loop(0, CHIPS)
        def _(other):
            relay(other).wait_recv()

        @pl.loop(0, CHIPS)
        def _(q):
            for h in range(NCH // 2):
                rows = pl.ds(2 * SUB * h, 2 * SUB)
                even = gathered[2 * q, rows].astype(F32)
                odd = gathered[2 * q + 1, rows].astype(F32)
                out = pl.ds(aligned(2 * SUB * q, 2 * SUB), 2 * SUB)
                ordered[2 * h, out] = jnp.concatenate([even[:SUB], odd[:SUB]], axis=0).astype(BF)
                ordered[2 * h + 1, out] = jnp.concatenate([even[SUB:], odd[SUB:]], axis=0).astype(BF)

    @pl.loop(0, 2)
    def _(p):
        down(p)

    @pl.loop(0, NCH)
    def _(s):
        @pl.when(s < 2)
        def _():
            fold(0, s)

        tangent(s)

        @pl.when(s >= 2)
        def _():
            fold(1, s - 2)

    gather_tokens()
    order_tokens()

    @pl.loop(0, NCH)
    def _(s):
        primal(s)

        @pl.when(s < 2)
        def _():
            fold(1, s + 2)

        @pl.when(s >= 2)
        def _():
            fold(2, s - 2)

    fold(2, 2)

    def ag1(k, side):
        block = terms.at[k, :, pl.ds(aligned(OWN * col, OWN), OWN)]
        return remote(block, block, ag1_send.at[side, k], ag1_recv.at[side, k], {"col": sides[side]})

    def ag2(k, side):
        rows = pl.ds(aligned(OWN * sides[1 - side] + HALF * side, HALF), HALF)
        block = terms.at[k, :, rows]
        return remote(block, block, ag2_send.at[side, k], ag2_recv.at[side, k], {"col": sides[side]})

    def work_terms(k):
        for side in range(2):
            rs2(1, k, side).wait_recv()
            rs2(2, k, side).wait_recv()

        @pl.when(lax.rem(k, 2) == 0)
        def _():
            for side in range(2):
                rs2(0, k // 2, side).wait_recv()

        rows = pl.ds(aligned(OWN * col, OWN), OWN)

        def full(part, red, start):
            cols = pl.ds(start, 128)
            return part[k, rows, cols].astype(F32) + red[0, k, :, cols].astype(F32) + red[1, k, :, cols].astype(F32)

        for start in range(0, HI, 128):
            gate_tan = full(part1, red1, start)
            up_tan = full(part1, red1, HI + start)
            down_back = full(part0, red0, start)
            gate_pre = full(part2, red2, start)
            up_pre = full(part2, red2, HI + start)
            sig = 1.0 / (1.0 + jnp.exp(-gate_pre))
            rest = 1.0 - sig
            first = sig * (1.0 + gate_pre * rest)
            second = sig * rest * (2.0 + gate_pre * (1.0 - 2.0 * sig))
            down_first = down_back * first
            terms[k, 0, rows, pl.ds(start, 128)] = (down_first * up_pre).astype(BF)
            terms[k, 0, rows, pl.ds(HI + start, 128)] = (down_back * gate_pre * sig).astype(BF)
            terms[k, 1, rows, pl.ds(start, 128)] = (
                down_back * (up_tan * first + up_pre * second * gate_tan)
            ).astype(BF)
            terms[k, 1, rows, pl.ds(HI + start, 128)] = (down_first * gate_tan).astype(BF)
        for side in range(2):
            ag1(k, side).start()

    def forward_terms(k):
        for side in range(2):
            ag1(k, side).wait_recv()
            ag2(k, side).start()

    def pair(k, h):
        return remote(
            pair_out.at[k, h], pair_in.at[k, h], pair_send.at[k, h], pair_recv.at[k, h], {"row": sib}
        )

    def row_copy(k, h, step):
        other, where = peer(step)
        return remote(
            row_out.at[k, h, other], row_in.at[k, h, chip],
            row_send.at[k, h, other], row_recv.at[k, h, chip], {"row": where},
        )

    def row_wait(k, h, other):
        return remote(
            row_out.at[k, h, other], row_in.at[k, h, other],
            row_send.at[k, h, other], row_recv.at[k, h, other], {"row": sib},
        )

    dsum[...] = jnp.zeros_like(dsum)

    def backward(k):
        for side in range(2):
            ag2(k, side).wait_recv()
        slot = lax.rem(k, 2)

        @pl.loop(0, 2)
        def _(h):
            cols = pl.ds(aligned(h * FH, FH), FH)
            res[...] = lax.dot_general(
                terms[k].reshape(2 * CT, HI2), w[cols, :], NT, preferred_element_type=F32
            )
            prod = res[CT:, :] * signs[k, :, cols].astype(F32)
            dsum[:, cols] += jnp.sum(prod.reshape(CT // 8, 8, FH), axis=0)

            @pl.loop(0, CHIPS)
            def _(m):
                rows = pl.ds(aligned(2 * SUB * m, 2 * SUB), 2 * SUB)
                for keep, at in ((False, 1 - core), (True, core)):
                    first = aligned(2 * SUB * m + SUB * at, SUB)
                    both = jnp.concatenate(
                        [res[pl.ds(first, SUB), :], res[pl.ds(aligned(CT + first, SUB), SUB), :]], axis=0
                    )
                    if keep:
                        mine[slot, h, rows] = both
                    else:
                        pair_out[k, h, rows] = both.astype(BF)

            pair(k, h).start()

    def send_rows(k):
        slot = lax.rem(k, 2)

        @pl.loop(0, 2)
        def _(h):
            pair(k, h).wait_recv()

            @pl.loop(0, CHIPS)
            def _(m):
                rows = pl.ds(aligned(2 * SUB * m, 2 * SUB), 2 * SUB)
                row_out[k, h, m] = (mine[slot, h, rows] + pair_in[k, h, rows].astype(F32)).astype(BF)

            @pl.loop(1, CHIPS)
            def _(step):
                row_copy(k, h, step).start()

            row_in[k, h, chip] = row_out[k, h, chip]

    def finish(k):
        rows = pl.ds(aligned(SUB * k, SUB), SUB)
        for h in range(2):

            @pl.loop(1, CHIPS)
            def _(step):
                row_wait(k, h, peer(step)[0]).wait_recv()

            total_k = row_in[k, h, 0].astype(F32)
            for m in range(1, CHIPS):
                total_k = total_k + row_in[k, h, m].astype(F32)
            cols = pl.ds(h * FH, FH)
            total[0, rows, cols] = total_k[:SUB]
            total[1, rows, cols] = total_k[SUB:]

    def d1(step):
        other, where = peer(step)
        return remote(dbuf1.at[chip], dbuf1.at[chip], d1_send.at[other], d1_recv.at[chip], {"row": where})

    def d1_wait(other):
        return remote(dbuf1.at[other], dbuf1.at[other], d1_send.at[other], d1_recv.at[other], {"row": sib})

    quad = 2 * rep + core

    def d2(which):
        where = ({"row": sib}, {"rep": 1 - rep}, {"rep": 1 - rep, "row": sib})[which]
        return remote(dbuf2.at[quad], dbuf2.at[quad], d2_send.at[which], d2_recv.at[which], where)

    @pl.loop(0, NCH + 4)
    def _(s):
        @pl.when(s < NCH)
        def _():
            work_terms(s)

        @pl.when(s == 0)
        def _():
            fold(2, NCH - 1)

        @pl.when(jnp.logical_and(s >= 1, s < NCH + 1))
        def _():
            forward_terms(s - 1)

        @pl.when(jnp.logical_and(s >= 3, s < NCH + 3))
        def _():
            send_rows(s - 3)

        @pl.when(jnp.logical_and(s >= 2, s < NCH + 2))
        def _():
            backward(s - 2)

        @pl.when(s == NCH + 1)
        def _():
            dbuf1[chip] = jnp.sum(dsum[...], axis=0, keepdims=True)
            for step in range(1, CHIPS):
                d1(step).start()

        @pl.when(s == NCH + 2)
        def _():
            for step in range(1, CHIPS):
                d1_wait(peer(step)[0]).wait_recv()
            dbuf2[quad] = jnp.sum(dbuf1[...], axis=0)
            for which in range(3):
                d2(which).start()

        @pl.when(s >= 4)
        def _():
            finish(s - 4)

    for which in range(3):
        d2(which).wait_recv()
    diag_out[...] = jnp.sum(dbuf2[...], axis=0) * (1.0 / (REPS * ROWS * NCH * SUB))

    own_to_sib().wait_send()
    for which in range(3):
        d2(which).wait_send()

    @pl.loop(1, CHIPS)
    def _(step):
        send_tok(step).wait_send()
        relay(peer(step)[0]).wait_send()
        d1(step).wait_send()

    @pl.loop(0, NCH)
    def _(k):
        for side in range(2):
            for batch in (1, 2):
                rs1(batch, k, side).wait_send()
                rs2(batch, k, side).wait_send()
            ag1(k, side).wait_send()
            ag2(k, side).wait_send()
        for h in range(2):
            pair(k, h).wait_send()

            @pl.loop(1, CHIPS)
            def _(step):
                row_copy(k, h, step).wait_send()

    @pl.loop(0, NCH // 2)
    def _(p):
        for side in range(2):
            rs1(0, p, side).wait_send()
            rs2(0, p, side).wait_send()


def write_out(total, diag, grad_out, hess_out, diag_out):
    grad_out[...] = total[0].astype(BF)
    hess_out[...] = total[1].astype(BF)
    diag_out[...] = diag[...]


def local(tokens, probe_bits, cot_codes, cot_scales, w_gate, w_up, w_down):
    split = (ROWS, NCH, SUB)
    vm = pl.BlockSpec(memory_space=pltpu.VMEM)
    hbm = pl.BlockSpec(memory_space=pl.ANY)
    dma = pltpu.SemaphoreType.DMA
    total, diag = pl.pallas_call(
        kernel,
        out_shape=(
            jax.ShapeDtypeStruct((2, NCH * SUB, FE), F32),
            jax.ShapeDtypeStruct((1, FE), F32),
        ),
        in_specs=[vm] + [hbm] * 6,
        out_specs=[vm] * 2,
        scratch_shapes=[
            pltpu.VMEM((FE, HI2), BF),
            pltpu.VMEM((HI, FE), BF),
            pltpu.VMEM((NCH, ROWS, SUB, FE), jnp.int32),
            pltpu.VMEM((NCH, ROWS, SUB, FE), jnp.int32),
            pltpu.VMEM((FE // 32, NCH * CT), jnp.int32),
            pltpu.VMEM((FE // 32, FE), BF),
            pltpu.VMEM((NCH * CT, FE // 32), BF),
            pltpu.VMEM((NCH, CT, FE), BF),
            pltpu.VMEM((2 * CT, FE), BF),
            pltpu.VMEM((ROWS, NCH * SUB, FE), BF),
            pltpu.VMEM((NCH, CT, FE), BF),
            pltpu.VMEM((NCH, CT, HI), BF),
            pltpu.VMEM((NCH, CT, HI2), BF),
            pltpu.VMEM((NCH, CT, HI2), BF),
            pltpu.VMEM((2, NCH, HALF, HI), BF),
            pltpu.VMEM((2, NCH, HALF, HI2), BF),
            pltpu.VMEM((2, NCH, HALF, HI2), BF),
            pltpu.VMEM((2, NCH, OWN, HI), BF),
            pltpu.VMEM((2, NCH, OWN, HI2), BF),
            pltpu.VMEM((2, NCH, OWN, HI2), BF),
            pltpu.VMEM((NCH, 2, CT, HI2), BF),
            pltpu.VMEM((2, 2, CT, FH), F32),
            pltpu.VMEM((NCH, 2, CT, FH), BF),
            pltpu.VMEM((NCH, 2, CT, FH), BF),
            pltpu.VMEM((NCH, 2, CHIPS, 2 * SUB, FH), BF),
            pltpu.VMEM((NCH, 2, CHIPS, 2 * SUB, FH), BF),
            pltpu.VMEM((8, FE), F32),
            pltpu.VMEM((CHIPS, 1, FE), F32),
            pltpu.VMEM((4, 1, FE), F32),
            pltpu.VMEM((2 * CT, FH), F32),
            dma((2 * NCH + 4,)),
            dma((CHIPS,)), dma((CHIPS,)), dma((CHIPS,)), dma((CHIPS,)),
            dma((2, 2 * NCH + 2)), dma((2, 2 * NCH + 2)), dma((2, 2 * NCH + 2)), dma((2, 2 * NCH + 2)),
            dma((2, NCH)), dma((2, NCH)), dma((2, NCH)), dma((2, NCH)),
            dma((NCH, 2)), dma((NCH, 2)),
            dma((NCH, 2, CHIPS)), dma((NCH, 2, CHIPS)),
            dma((CHIPS,)), dma((CHIPS,)), dma((3,)), dma((3,)),
        ],
        compiler_params=pltpu.CompilerParams(
            collective_id=0, has_side_effects=True, vmem_limit_bytes=63 * 2**20
        ),
    )(
        tokens,
        probe_bits.reshape(split + (FE,)),
        cot_codes.reshape(split + (FE,)),
        cot_scales.T,
        w_gate,
        w_up,
        w_down,
    )
    return pl.pallas_call(
        write_out,
        out_shape=(
            jax.ShapeDtypeStruct((NCH * SUB, FE), BF),
            jax.ShapeDtypeStruct((NCH * SUB, FE), BF),
            jax.ShapeDtypeStruct((FE,), F32),
        ),
        in_specs=[vm] * 2,
        out_specs=[vm] * 3,
    )(total, diag.reshape(FE))


def solution(mesh):
    in_specs = (
        P(("rep", "row"), "col"),
        P("rep", "col"),
        P("rep", "col"),
        P("rep", "col"),
        P("col", "row"),
        P("col", "row"),
        P("row", "col"),
    )
    out_specs = (P(("rep", "row"), "col"), P(("rep", "row"), "col"), P("col"))
    return jax.shard_map(local, mesh=mesh, in_specs=in_specs, out_specs=out_specs, check_vma=False)
```

```python
import functools

import jax
import jax.numpy as jnp
from jax import lax
from jax.experimental import pallas as pl
from jax.experimental.pallas import tpu as pltpu
from jax.sharding import PartitionSpec as P

MESH = pl.DeviceIdType.MESH
BF = jnp.bfloat16
F32 = jnp.float32
REPS, ROWS, COLS = 2, 16, 4
CHIPS = ROWS // 2
ZS = CHIPS // 2
NEAR = ((1, 0), (3, 0))
MID = ((2, 0), (0, 1))
FAR = ((1, 1), (3, 1), (2, 1))
ALL = FAR[::-1] + MID + NEAR
NCH = 4
SUB = 8
CT = ROWS * SUB
OWN = CT // COLS
HALF = OWN // 2
FE = 2048
HI = 896
HI2 = 2 * HI
FH = FE // 2
NT = (((1,), (1,)), ((), ()))


def aligned(value, step):
    return pl.multiple_of(value, step)


def kernel(
    tok, bits_hbm, codes_hbm, scales_hbm, wg_hbm, wu_hbm, wd_hbm,
    both_out, diag_out,
    w, wd, bits, codes, scales, spread, power, signs, cot, gathered, ordered,
    part0, part1, part2, in0, in1, in2, red0, red1, red2, terms, total, mine,
    pair_out, pair_in, row_out, row_in, dsum, dbuf1, dbuf2, res,
    load_sem, send_sem, tok_recv, sib_recv, rs1_recv, rs2_recv, ag1_recv, ag2_recv,
    pair_recv, row_recv, d1_recv, d2_recv, ready,
):
    rep = lax.axis_index("rep")
    row = lax.axis_index("row")
    col = lax.axis_index("col")
    core = lax.rem(row, 2)
    chip = row // 2
    sib = row + 1 - 2 * core
    left = lax.rem(col + COLS - 1, COLS)
    right = lax.rem(col + 1, COLS)
    opp = lax.rem(col + 2, COLS)
    sides = (left, right)

    z, xh = chip // 2, lax.rem(chip, 2)

    def peer(away):
        other = lax.rem(z + away[0], ZS) * 2 + lax.rem(xh + away[1], 2)
        return other, 2 * other + core

    def load_bits(k):
        return pltpu.make_async_copy(bits_hbm.at[:, k], bits.at[k], load_sem.at[k])

    def load_codes(k):
        return pltpu.make_async_copy(codes_hbm.at[:, k], codes.at[k], load_sem.at[NCH + k])

    load_wg = pltpu.make_async_copy(wg_hbm, w.at[:, pl.ds(0, HI)], load_sem.at[2 * NCH])
    load_wu = pltpu.make_async_copy(wu_hbm, w.at[:, pl.ds(HI, HI)], load_sem.at[2 * NCH + 1])
    load_wd = pltpu.make_async_copy(wd_hbm, wd, load_sem.at[2 * NCH + 2])
    load_sc = pltpu.make_async_copy(scales_hbm, scales, load_sem.at[2 * NCH + 3])
    load_tok = pltpu.make_async_copy(tok, gathered.at[row], load_sem.at[2 * NCH + 4])
    load_sc.start()
    load_codes(0).start()
    load_codes(1).start()
    load_tok.start()
    load_wd.start()
    load_codes(2).start()
    load_codes(3).start()
    load_bits(0).start()
    load_wg.start()
    load_wu.start()
    for k in range(1, NCH):
        load_bits(k).start()

    barrier = pltpu.get_barrier_semaphore()

    def tell(sem, where):
        pl.semaphore_signal(sem, inc=1, device_id=where, device_id_type=MESH)

    opposite_row = peer((0, 1))[1]
    for side in sides:
        tell(barrier, {"col": side})
    tell(barrier, {"row": sib})
    for away in NEAR:
        tell(barrier, {"row": peer(away)[1]})
    for other_row in (row, sib, opposite_row):
        tell(barrier, {"rep": 1 - rep, "row": other_row})

    def enter_first():
        pl.semaphore_wait(barrier, 8)
        for away in NEAR:
            tell(ready.at[0], {"row": peer(away)[1]})
        tell(ready.at[0], {"rep": 1 - rep})

    def enter_second():
        pl.semaphore_wait(ready.at[0], 3)
        tell(ready.at[1], {"row": opposite_row})

    def enter_third():
        pl.semaphore_wait(ready.at[1], 1)

    def remote(src, dst, recv, where):
        return pltpu.make_async_remote_copy(
            src_ref=src, dst_ref=dst, send_sem=send_sem.at[0], recv_sem=recv, device_id=where, device_id_type=MESH
        )

    def arrived(block, recv):
        remote(block, block, recv, {"row": sib}).wait_recv()

    def sent(block):
        remote(block, block, tok_recv.at[0], {"row": sib}).wait_send()

    across = (0, 1)
    column = NEAR + ((2, 0),)

    def send_tok(block_row, where, recv):
        block = gathered.at[block_row]
        return remote(block, block, recv, {"row": where})

    def own_tok(away):
        return send_tok(row, peer(away)[1], tok_recv.at[0 if away == across else 1])

    def onward_tok(away):
        return send_tok(opposite_row, peer(away)[1], tok_recv.at[1])

    def share_tok(block_row):
        return send_tok(block_row, sib, sib_recv.at[0])

    lanes = lax.broadcasted_iota(jnp.int32, spread.shape, 1) // 32
    spread[...] = (lanes == lax.broadcasted_iota(jnp.int32, spread.shape, 0)).astype(F32).astype(BF)
    at = lax.broadcasted_iota(jnp.int32, (NCH * CT, NCH * CT), 0)
    token = (at % CT) // SUB * (NCH * SUB) + at // CT * SUB + at % SUB
    pick = (token == lax.broadcasted_iota(jnp.int32, (NCH * CT, NCH * CT), 1)).astype(F32).astype(BF)
    load_sc.wait()
    raised = (lax.shift_left(1, scales[...] + 2).astype(F32) * 2.0**-7).astype(BF)
    power[...] = lax.dot_general(pick, raised, NT, preferred_element_type=F32).astype(BF)

    batches = ((part0, in0, red0, 2, 0), (part1, in1, red1, 1, 2), (part2, in2, red2, 1, 2 + NCH))

    def rs1(batch, k, side):
        part, inn, _, n, base = batches[batch]
        ks = pl.ds(k * n, n)
        src = part.at[ks, pl.ds(aligned(OWN * opp + HALF * side, HALF), HALF)]
        return remote(src, inn.at[side, ks], rs1_recv.at[base + k], {"col": sides[side]})

    def rs2(batch, k, side):
        part, _, red, n, base = batches[batch]
        ks = pl.ds(k * n, n)
        src = part.at[ks, pl.ds(aligned(OWN * sides[side], OWN), OWN)]
        return remote(src, red.at[side, ks], rs2_recv.at[base + k], {"col": sides[side]})

    def start_rs1(batch, k):
        for side in range(2):
            rs1(batch, k, side).start()

    def fold(batch, k):
        part, inn, _, n, base = batches[batch]
        arrived(inn.at[:, pl.ds(k * n, n)], rs1_recv.at[base + k])
        for side in range(2):
            rows = pl.ds(aligned(OWN * sides[side] + HALF * side, HALF), HALF)
            for i in range(n):
                at = k * n + i
                part[at, rows] = (part[at, rows].astype(F32) + inn[side, at].astype(F32)).astype(BF)
            rs2(batch, k, side).start()

    def folded(batch, k):
        _, _, red, n, base = batches[batch]
        arrived(red.at[:, pl.ds(k * n, n)], rs2_recv.at[base + k])

    def down(p):
        for i in range(2):
            load_codes(2 * p + i).wait()

        @pl.loop(0, FE // 512)
        def _(n):
            cols = pl.ds(aligned(n * 512, 512), 512)
            code = codes[pl.ds(2 * p, 2), :, :, cols].reshape(2 * CT, 512)
            size = lax.shift_left((code & 7) | 8, ((code >> 3) & 15) - 5)
            value = jnp.where(code >= 128, -size, size).astype(F32)
            wide = jnp.dot(
                power[pl.ds(aligned(2 * CT * p, 2 * CT), 2 * CT), :], spread[:, cols], preferred_element_type=F32
            )
            cot[:, cols] = (value * wide).astype(BF)

        if p == 0:
            load_wd.wait()

        part0[pl.ds(2 * p, 2)] = (
            lax.dot_general(cot[...], wd[...], NT, preferred_element_type=F32).astype(BF).reshape(2, CT, HI)
        )

    def tangent(k):
        load_bits(k).wait()
        signs[k] = (2 * bits[k].reshape(CT, FE) - 1).astype(F32).astype(BF)

        @pl.when(k == 0)
        def _():
            load_wg.wait()
            load_wu.wait()

        part1[k] = jnp.dot(signs[k], w[...], preferred_element_type=F32).astype(BF)
        start_rs1(1, k)

    def primal(k):
        part2[k] = jnp.dot(ordered[k], w[...], preferred_element_type=F32).astype(BF)
        start_rs1(2, k)

    def onward_tokens():
        arrived(gathered.at[opposite_row], tok_recv.at[0])
        for away in column:
            onward_tok(away).start()
        share_tok(opposite_row).start()

    def gather_tokens():
        arrived(gathered.at[pl.ds(0, 6)], tok_recv.at[1])
        for away in column:
            other, where = peer(away)
            share_tok(where).start()
            share_tok(peer((away[0], 1))[1]).start()

    def order_tokens():
        arrived(gathered.at[pl.ds(0, CHIPS)], sib_recv.at[0])

        @pl.loop(0, CHIPS)
        def _(q):
            for h in range(NCH // 2):
                rows = pl.ds(2 * SUB * h, 2 * SUB)
                even = gathered[2 * q, rows].astype(F32)
                odd = gathered[2 * q + 1, rows].astype(F32)
                out = pl.ds(aligned(2 * SUB * q, 2 * SUB), 2 * SUB)
                ordered[2 * h, out] = jnp.concatenate([even[:SUB], odd[:SUB]], axis=0).astype(BF)
                ordered[2 * h + 1, out] = jnp.concatenate([even[SUB:], odd[SUB:]], axis=0).astype(BF)

    down(0)
    enter_first()
    start_rs1(0, 0)
    load_tok.wait()
    for away in NEAR:
        own_tok(away).start()
    share_tok(row).start()
    down(1)
    start_rs1(0, 1)
    enter_second()
    own_tok(across).start()
    own_tok((2, 0)).start()
    fold(0, 0)

    @pl.loop(0, NCH)
    def _(s):
        tangent(s)

        @pl.when(s == 0)
        def _():
            fold(0, 1)

        @pl.when(s == 1)
        def _():
            onward_tokens()

        @pl.when(s >= 2)
        def _():
            fold(1, s - 2)

    gather_tokens()
    order_tokens()
    enter_third()

    @pl.loop(0, NCH)
    def _(s):
        primal(s)

        @pl.when(s < 2)
        def _():
            fold(1, s + 2)

        @pl.when(s >= 2)
        def _():
            fold(2, s - 2)

    fold(2, 2)

    def ag1(k, side):
        block = terms.at[k, :, pl.ds(aligned(OWN * col, OWN), OWN)]
        return remote(block, block, ag1_recv.at[k], {"col": sides[side]})

    def ag2(k, side):
        rows = pl.ds(aligned(OWN * sides[1 - side] + HALF * side, HALF), HALF)
        block = terms.at[k, :, rows]
        return remote(block, block, ag2_recv.at[k], {"col": sides[side]})

    def work_terms(k):
        folded(1, k)
        folded(2, k)

        @pl.when(lax.rem(k, 2) == 0)
        def _():
            folded(0, k // 2)

        rows = pl.ds(aligned(OWN * col, OWN), OWN)

        def full(part, red, start):
            cols = pl.ds(start, 128)
            return part[k, rows, cols].astype(F32) + red[0, k, :, cols].astype(F32) + red[1, k, :, cols].astype(F32)

        for start in range(0, HI, 128):
            gate_tan = full(part1, red1, start)
            up_tan = full(part1, red1, HI + start)
            down_back = full(part0, red0, start)
            gate_pre = full(part2, red2, start)
            up_pre = full(part2, red2, HI + start)
            sig = 1.0 / (1.0 + jnp.exp(-gate_pre))
            rest = 1.0 - sig
            first = sig * (1.0 + gate_pre * rest)
            second = sig * rest * (2.0 + gate_pre * (1.0 - 2.0 * sig))
            down_first = down_back * first
            terms[k, 0, rows, pl.ds(start, 128)] = (down_first * up_pre).astype(BF)
            terms[k, 0, rows, pl.ds(HI + start, 128)] = (down_back * gate_pre * sig).astype(BF)
            terms[k, 1, rows, pl.ds(start, 128)] = (
                down_back * (up_tan * first + up_pre * second * gate_tan)
            ).astype(BF)
            terms[k, 1, rows, pl.ds(HI + start, 128)] = (down_first * gate_tan).astype(BF)
        for side in range(2):
            ag1(k, side).start()

    def forward_terms(k):
        arrived(terms.at[k, :, pl.ds(0, 2 * OWN)], ag1_recv.at[k])
        for side in range(2):
            ag2(k, side).start()

    def pair(k, h):
        return remote(pair_out.at[k, h], pair_in.at[k, h], pair_recv.at[k, h], {"row": sib})

    def row_copy(k, h, away):
        other, where = peer(away)
        return remote(row_out.at[k, h, other], row_in.at[k, h, chip], row_recv.at[k, h], {"row": where})

    dsum[...] = jnp.zeros_like(dsum)

    def backward(k):
        arrived(terms.at[k, :, pl.ds(0, OWN)], ag2_recv.at[k])
        slot = lax.rem(k, 2)

        @pl.loop(0, 2)
        def _(h):
            cols = pl.ds(aligned(h * FH, FH), FH)
            res[...] = lax.dot_general(
                terms[k].reshape(2 * CT, HI2), w[cols, :], NT, preferred_element_type=F32
            )
            prod = res[CT:, :] * signs[k, :, cols].astype(F32)
            dsum[:, cols] += jnp.sum(prod.reshape(CT // 8, 8, FH), axis=0)

            @pl.loop(0, CHIPS)
            def _(m):
                rows = pl.ds(aligned(2 * SUB * m, 2 * SUB), 2 * SUB)
                for keep, at in ((False, 1 - core), (True, core)):
                    first = aligned(2 * SUB * m + SUB * at, SUB)
                    both = jnp.concatenate(
                        [res[pl.ds(first, SUB), :], res[pl.ds(aligned(CT + first, SUB), SUB), :]], axis=0
                    )
                    if keep:
                        mine[slot, h, rows] = both
                    else:
                        pair_out[k, h, rows] = both.astype(BF)

            pair(k, h).start()

    def send_rows(k):
        slot = lax.rem(k, 2)

        @pl.loop(0, 2)
        def _(h):
            pair(k, h).wait_recv()

            @pl.loop(0, CHIPS)
            def _(m):
                rows = pl.ds(aligned(2 * SUB * m, 2 * SUB), 2 * SUB)
                row_out[k, h, m] = (mine[slot, h, rows] + pair_in[k, h, rows].astype(F32)).astype(BF)

            for away in ALL:
                row_copy(k, h, away).start()

            row_in[k, h, chip] = row_out[k, h, chip]

    def finish(k):
        rows = pl.ds(aligned(SUB * k, SUB), SUB)
        for h in range(2):
            arrived(row_in.at[k, h, pl.ds(0, CHIPS - 1)], row_recv.at[k, h])

            total_k = row_in[k, h, 0].astype(F32)
            for m in range(1, CHIPS):
                total_k = total_k + row_in[k, h, m].astype(F32)
            cols = pl.ds(h * FH, FH)
            total[0, rows, cols] = total_k[:SUB]
            total[1, rows, cols] = total_k[SUB:]

    def d1(away):
        return remote(dbuf1.at[chip], dbuf1.at[chip], d1_recv.at[0], {"row": peer(away)[1]})

    quad = 2 * rep + core

    def d2(which):
        where = ({"row": sib}, {"rep": 1 - rep}, {"rep": 1 - rep, "row": sib})[which]
        return remote(dbuf2.at[quad], dbuf2.at[quad], d2_recv.at[0], where)

    @pl.loop(0, NCH + 4)
    def _(s):
        @pl.when(s < NCH)
        def _():
            work_terms(s)

        @pl.when(s == 0)
        def _():
            fold(2, NCH - 1)

        @pl.when(jnp.logical_and(s >= 1, s < NCH + 1))
        def _():
            forward_terms(s - 1)

        @pl.when(jnp.logical_and(s >= 3, s < NCH + 3))
        def _():
            send_rows(s - 3)

        @pl.when(jnp.logical_and(s >= 2, s < NCH + 2))
        def _():
            backward(s - 2)

        @pl.when(s == NCH + 1)
        def _():
            dbuf1[chip] = jnp.sum(dsum[...], axis=0, keepdims=True)
            for away in ALL:
                d1(away).start()

        @pl.when(s == NCH + 2)
        def _():
            arrived(dbuf1.at[pl.ds(0, CHIPS - 1)], d1_recv.at[0])
            dbuf2[quad] = jnp.sum(dbuf1[...], axis=0)
            for which in range(3):
                d2(which).start()

        @pl.when(s >= 4)
        def _():
            finish(s - 4)

    both_out[...] = total[...].astype(BF)
    arrived(dbuf2.at[pl.ds(0, 3)], d2_recv.at[0])
    diag_out[...] = jnp.sum(dbuf2[...], axis=0) * (1.0 / (REPS * ROWS * NCH * SUB))

    for block in (in0, in1, in2, red0, red1, red2, pair_out):
        sent(block)
    sent(gathered.at[pl.ds(0, CHIPS - 1)])
    sent(gathered.at[pl.ds(0, CHIPS)])
    sent(terms.at[:, :, pl.ds(0, 2 * OWN)])
    sent(terms.at[:, :, pl.ds(0, OWN)])
    sent(row_out.at[:, :, pl.ds(0, CHIPS - 1)])
    sent(dbuf1.at[pl.ds(0, CHIPS - 1)])
    sent(dbuf2.at[pl.ds(0, 3)])


def write_out(total, diag, grad_out, hess_out, diag_out):
    grad_out[...] = total[0]
    hess_out[...] = total[1]
    diag_out[...] = diag[...]


def local(tokens, probe_bits, cot_codes, cot_scales, w_gate, w_up, w_down):
    split = (ROWS, NCH, SUB)
    vm = pl.BlockSpec(memory_space=pltpu.VMEM)
    hbm = pl.BlockSpec(memory_space=pl.ANY)
    dma = pltpu.SemaphoreType.DMA
    total, diag = pl.pallas_call(
        kernel,
        out_shape=(
            jax.ShapeDtypeStruct((2, NCH * SUB, FE), BF),
            jax.ShapeDtypeStruct((1, FE), F32),
        ),
        in_specs=[hbm] * 7,
        out_specs=[vm] * 2,
        scratch_shapes=[
            pltpu.VMEM((FE, HI2), BF),
            pltpu.VMEM((HI, FE), BF),
            pltpu.VMEM((NCH, ROWS, SUB, FE), jnp.int32),
            pltpu.VMEM((NCH, ROWS, SUB, FE), jnp.int32),
            pltpu.VMEM((FE // 32, NCH * CT), jnp.int32),
            pltpu.VMEM((FE // 32, FE), BF),
            pltpu.VMEM((NCH * CT, FE // 32), BF),
            pltpu.VMEM((NCH, CT, FE), BF),
            pltpu.VMEM((2 * CT, FE), BF),
            pltpu.VMEM((ROWS, NCH * SUB, FE), BF),
            pltpu.VMEM((NCH, CT, FE), BF),
            pltpu.VMEM((NCH, CT, HI), BF),
            pltpu.VMEM((NCH, CT, HI2), BF),
            pltpu.VMEM((NCH, CT, HI2), BF),
            pltpu.VMEM((2, NCH, HALF, HI), BF),
            pltpu.VMEM((2, NCH, HALF, HI2), BF),
            pltpu.VMEM((2, NCH, HALF, HI2), BF),
            pltpu.VMEM((2, NCH, OWN, HI), BF),
            pltpu.VMEM((2, NCH, OWN, HI2), BF),
            pltpu.VMEM((2, NCH, OWN, HI2), BF),
            pltpu.VMEM((NCH, 2, CT, HI2), BF),
            pltpu.VMEM((2, NCH * SUB, FE), F32),
            pltpu.VMEM((2, 2, CT, FH), F32),
            pltpu.VMEM((NCH, 2, CT, FH), BF),
            pltpu.VMEM((NCH, 2, CT, FH), BF),
            pltpu.VMEM((NCH, 2, CHIPS, 2 * SUB, FH), BF),
            pltpu.VMEM((NCH, 2, CHIPS, 2 * SUB, FH), BF),
            pltpu.VMEM((8, FE), F32),
            pltpu.VMEM((CHIPS, 1, FE), F32),
            pltpu.VMEM((4, 1, FE), F32),
            pltpu.VMEM((2 * CT, FH), F32),
            dma((2 * NCH + 5,)), dma((1,)),
            dma((2,)), dma((1,)),
            dma((2 * NCH + 2,)), dma((2 * NCH + 2,)),
            dma((NCH,)), dma((NCH,)),
            dma((NCH, 2)), dma((NCH, 2)),
            dma((1,)), dma((1,)),
            pltpu.SemaphoreType.REGULAR((2,)),
        ],
        compiler_params=pltpu.CompilerParams(
            collective_id=0, has_side_effects=True, vmem_limit_bytes=63 * 2**20
        ),
    )(
        tokens,
        probe_bits.reshape(split + (FE,)),
        cot_codes.reshape(split + (FE,)),
        cot_scales.T,
        w_gate,
        w_up,
        w_down,
    )
    return pl.pallas_call(
        write_out,
        out_shape=(
            jax.ShapeDtypeStruct((NCH * SUB, FE), BF),
            jax.ShapeDtypeStruct((NCH * SUB, FE), BF),
            jax.ShapeDtypeStruct((FE,), F32),
        ),
        in_specs=[vm] * 2,
        out_specs=[vm] * 3,
    )(total, diag.reshape(FE))


def solution(mesh):
    in_specs = (
        P(("rep", "row"), "col"),
        P("rep", "col"),
        P("rep", "col"),
        P("rep", "col"),
        P("col", "row"),
        P("col", "row"),
        P("row", "col"),
    )
    out_specs = (P(("rep", "row"), "col"), P(("rep", "row"), "col"), P("col"))
    return jax.shard_map(local, mesh=mesh, in_specs=in_specs, out_specs=out_specs, check_vma=False)
```

```python
import functools

import jax
import jax.numpy as jnp
from jax import lax
from jax.experimental import pallas as pl
from jax.experimental.pallas import tpu as pltpu
from jax.sharding import PartitionSpec as P

MESH = pl.DeviceIdType.MESH
BF = jnp.bfloat16
F32 = jnp.float32
REPS, ROWS, COLS = 2, 16, 4
CHIPS = ROWS // 2
ZS = CHIPS // 2
NEAR = ((1, 0), (3, 0))
MID = ((2, 0), (0, 1))
FAR = ((1, 1), (3, 1), (2, 1))
ALL = FAR[::-1] + MID + NEAR
NCH = 4
SUB = 8
CT = ROWS * SUB
OWN = CT // COLS
HALF = OWN // 2
FE = 2048
HI = 896
HI2 = 2 * HI
FH = FE // 2
NT = (((1,), (1,)), ((), ()))


def aligned(value, step):
    return pl.multiple_of(value, step)


def kernel(
    tok, bits_hbm, codes_hbm, scales_hbm, wg_hbm, wu_hbm, wd_hbm,
    both_out, diag_out,
    w, wd, bits, codes, scales, spread, power, signs, cot, gathered, ordered,
    part0, part1, part2, in0, in1, in2, red0, red1, red2, terms, total, mine,
    pair_out, pair_in, row_out, row_in, dsum, dbuf1, dbuf2, res,
    load_sem, send_sem, tok_recv, sib_recv, rs1_recv, rs2_recv, ag1_recv, ag2_recv,
    pair_recv, row_recv, d1_recv, d2_recv, ready,
):
    rep = lax.axis_index("rep")
    row = lax.axis_index("row")
    col = lax.axis_index("col")
    core = lax.rem(row, 2)
    chip = row // 2
    sib = row + 1 - 2 * core
    left = lax.rem(col + COLS - 1, COLS)
    right = lax.rem(col + 1, COLS)
    opp = lax.rem(col + 2, COLS)
    sides = (left, right)

    z, xh = chip // 2, lax.rem(chip, 2)

    def peer(away):
        other = lax.rem(z + away[0], ZS) * 2 + lax.rem(xh + away[1], 2)
        return other, 2 * other + core

    def load_bits(k):
        return pltpu.make_async_copy(bits_hbm.at[:, k], bits.at[k], load_sem.at[k])

    def load_codes(k):
        return pltpu.make_async_copy(codes_hbm.at[:, k], codes.at[k], load_sem.at[NCH + k])

    load_wg = pltpu.make_async_copy(wg_hbm, w.at[:, pl.ds(0, HI)], load_sem.at[2 * NCH])
    load_wu = pltpu.make_async_copy(wu_hbm, w.at[:, pl.ds(HI, HI)], load_sem.at[2 * NCH + 1])
    load_wd = pltpu.make_async_copy(wd_hbm, wd, load_sem.at[2 * NCH + 2])
    load_sc = pltpu.make_async_copy(scales_hbm, scales, load_sem.at[2 * NCH + 3])
    load_tok = pltpu.make_async_copy(tok, gathered.at[row], load_sem.at[2 * NCH + 4])
    load_sc.start()
    load_codes(0).start()
    load_codes(1).start()
    load_tok.start()
    load_wd.start()
    load_codes(2).start()
    load_codes(3).start()
    load_bits(0).start()
    load_wg.start()
    load_wu.start()
    for k in range(1, NCH):
        load_bits(k).start()

    barrier = pltpu.get_barrier_semaphore()

    def tell(sem, where):
        pl.semaphore_signal(sem, inc=1, device_id=where, device_id_type=MESH)

    opposite_row = peer((0, 1))[1]
    for side in sides:
        tell(barrier, {"col": side})
    tell(barrier, {"row": sib})
    for away in NEAR:
        tell(barrier, {"row": peer(away)[1]})
    for other_row in (row, sib, opposite_row):
        tell(barrier, {"rep": 1 - rep, "row": other_row})

    def enter_first():
        pl.semaphore_wait(barrier, 8)
        for away in NEAR:
            tell(ready.at[0], {"row": peer(away)[1]})
        tell(ready.at[0], {"rep": 1 - rep})

    def enter_second():
        pl.semaphore_wait(ready.at[0], 3)
        tell(ready.at[1], {"row": opposite_row})

    def enter_third():
        pl.semaphore_wait(ready.at[1], 1)

    def remote(src, dst, recv, where):
        return pltpu.make_async_remote_copy(
            src_ref=src, dst_ref=dst, send_sem=send_sem.at[0], recv_sem=recv, device_id=where, device_id_type=MESH
        )

    def arrived(block, recv):
        remote(block, block, recv, {"row": sib}).wait_recv()

    def sent(block):
        remote(block, block, tok_recv.at[0], {"row": sib}).wait_send()

    across = (0, 1)
    column = NEAR + ((2, 0),)

    def send_tok(block_row, where, recv):
        block = gathered.at[block_row]
        return remote(block, block, recv, {"row": where})

    def own_tok(away):
        return send_tok(row, peer(away)[1], tok_recv.at[0 if away == across else 1])

    def onward_tok(away):
        return send_tok(opposite_row, peer(away)[1], tok_recv.at[1])

    def share_tok(block_row):
        return send_tok(block_row, sib, sib_recv.at[0])

    lanes = lax.broadcasted_iota(jnp.int32, spread.shape, 1) // 32
    spread[...] = (lanes == lax.broadcasted_iota(jnp.int32, spread.shape, 0)).astype(F32).astype(BF)
    at = lax.broadcasted_iota(jnp.int32, (NCH * CT, NCH * CT), 0)
    token = (at % CT) // SUB * (NCH * SUB) + at // CT * SUB + at % SUB
    pick = (token == lax.broadcasted_iota(jnp.int32, (NCH * CT, NCH * CT), 1)).astype(F32).astype(BF)
    load_sc.wait()
    raised = (lax.shift_left(1, scales[...] + 2).astype(F32) * 2.0**-7).astype(BF)
    power[...] = lax.dot_general(pick, raised, NT, preferred_element_type=F32).astype(BF)

    batches = ((part0, in0, red0, 2, 0), (part1, in1, red1, 1, 2), (part2, in2, red2, 1, 2 + NCH))

    def rs1(batch, k, side):
        part, inn, _, n, base = batches[batch]
        ks = pl.ds(k * n, n)
        src = part.at[ks, pl.ds(aligned(OWN * opp + HALF * side, HALF), HALF)]
        return remote(src, inn.at[side, ks], rs1_recv.at[base + k], {"col": sides[side]})

    def rs2(batch, k, side):
        part, _, red, n, base = batches[batch]
        ks = pl.ds(k * n, n)
        src = part.at[ks, pl.ds(aligned(OWN * sides[side], OWN), OWN)]
        return remote(src, red.at[side, ks], rs2_recv.at[base + k], {"col": sides[side]})

    def start_rs1(batch, k):
        for side in range(2):
            rs1(batch, k, side).start()

    def fold(batch, k):
        part, inn, _, n, base = batches[batch]
        arrived(inn.at[:, pl.ds(k * n, n)], rs1_recv.at[base + k])
        for side in range(2):
            rows = pl.ds(aligned(OWN * sides[side] + HALF * side, HALF), HALF)
            for i in range(n):
                at = k * n + i
                part[at, rows] = (part[at, rows].astype(F32) + inn[side, at].astype(F32)).astype(BF)
            rs2(batch, k, side).start()

    def folded(batch, k):
        _, _, red, n, base = batches[batch]
        arrived(red.at[:, pl.ds(k * n, n)], rs2_recv.at[base + k])

    def down(p):
        for i in range(2):
            load_codes(2 * p + i).wait()

        @pl.loop(0, FE // 512)
        def _(n):
            cols = pl.ds(aligned(n * 512, 512), 512)
            code = codes[pl.ds(2 * p, 2), :, :, cols].reshape(2 * CT, 512)
            size = lax.shift_left((code & 7) | 8, ((code >> 3) & 15) - 5)
            value = jnp.where(code >= 128, -size, size).astype(F32)
            wide = jnp.dot(
                power[pl.ds(aligned(2 * CT * p, 2 * CT), 2 * CT), :], spread[:, cols], preferred_element_type=F32
            )
            cot[:, cols] = (value * wide).astype(BF)

        if p == 0:
            load_wd.wait()

        part0[pl.ds(2 * p, 2)] = (
            lax.dot_general(cot[...], wd[...], NT, preferred_element_type=F32).astype(BF).reshape(2, CT, HI)
        )

    def tangent(k):
        load_bits(k).wait()
        signs[k] = (2 * bits[k].reshape(CT, FE) - 1).astype(F32).astype(BF)

        @pl.when(k == 0)
        def _():
            load_wg.wait()
            load_wu.wait()

        part1[k] = jnp.dot(signs[k], w[...], preferred_element_type=F32).astype(BF)
        start_rs1(1, k)

    def primal(k):
        part2[k] = jnp.dot(ordered[k], w[...], preferred_element_type=F32).astype(BF)
        start_rs1(2, k)

    def onward_tokens():
        arrived(gathered.at[opposite_row], tok_recv.at[0])
        for away in column:
            onward_tok(away).start()
        share_tok(opposite_row).start()

    def gather_tokens():
        arrived(gathered.at[pl.ds(0, 6)], tok_recv.at[1])
        for away in column:
            other, where = peer(away)
            share_tok(where).start()
            share_tok(peer((away[0], 1))[1]).start()

    def order_tokens():
        arrived(gathered.at[pl.ds(0, CHIPS)], sib_recv.at[0])

        @pl.loop(0, CHIPS)
        def _(q):
            for h in range(NCH // 2):
                rows = pl.ds(2 * SUB * h, 2 * SUB)
                even = gathered[2 * q, rows].astype(F32)
                odd = gathered[2 * q + 1, rows].astype(F32)
                out = pl.ds(aligned(2 * SUB * q, 2 * SUB), 2 * SUB)
                ordered[2 * h, out] = jnp.concatenate([even[:SUB], odd[:SUB]], axis=0).astype(BF)
                ordered[2 * h + 1, out] = jnp.concatenate([even[SUB:], odd[SUB:]], axis=0).astype(BF)

    down(0)
    enter_first()
    start_rs1(0, 0)
    load_tok.wait()
    for away in NEAR:
        own_tok(away).start()
    share_tok(row).start()
    down(1)
    start_rs1(0, 1)
    enter_second()
    own_tok(across).start()
    own_tok((2, 0)).start()
    fold(0, 0)

    @pl.loop(0, NCH)
    def _(s):
        tangent(s)

        @pl.when(s == 0)
        def _():
            fold(0, 1)

        @pl.when(s == 1)
        def _():
            onward_tokens()

        @pl.when(s >= 2)
        def _():
            fold(1, s - 2)

    gather_tokens()
    order_tokens()
    enter_third()

    @pl.loop(0, NCH)
    def _(s):
        primal(s)

        @pl.when(s < 2)
        def _():
            fold(1, s + 2)

        @pl.when(s >= 2)
        def _():
            fold(2, s - 2)

    fold(2, 2)

    def ag1(k, side, later):
        half = 1 - side if later else side
        block = terms.at[k, :, pl.ds(aligned(OWN * col + HALF * half, HALF), HALF)]
        return remote(block, block, ag1_recv.at[later, k], {"col": sides[side]})

    def ag2(k, side):
        rows = pl.ds(aligned(OWN * sides[1 - side] + HALF * side, HALF), HALF)
        block = terms.at[k, :, rows]
        return remote(block, block, ag2_recv.at[k], {"col": sides[side]})

    def work_terms(k):
        folded(1, k)
        folded(2, k)

        @pl.when(lax.rem(k, 2) == 0)
        def _():
            folded(0, k // 2)

        rows = pl.ds(aligned(OWN * col, OWN), OWN)

        def full(part, red, start):
            cols = pl.ds(start, 128)
            return part[k, rows, cols].astype(F32) + red[0, k, :, cols].astype(F32) + red[1, k, :, cols].astype(F32)

        for start in range(0, HI, 128):
            gate_tan = full(part1, red1, start)
            up_tan = full(part1, red1, HI + start)
            down_back = full(part0, red0, start)
            gate_pre = full(part2, red2, start)
            up_pre = full(part2, red2, HI + start)
            sig = 1.0 / (1.0 + jnp.exp(-gate_pre))
            rest = 1.0 - sig
            first = sig * (1.0 + gate_pre * rest)
            second = sig * rest * (2.0 + gate_pre * (1.0 - 2.0 * sig))
            down_first = down_back * first
            terms[k, 0, rows, pl.ds(start, 128)] = (down_first * up_pre).astype(BF)
            terms[k, 0, rows, pl.ds(HI + start, 128)] = (down_back * gate_pre * sig).astype(BF)
            terms[k, 1, rows, pl.ds(start, 128)] = (
                down_back * (up_tan * first + up_pre * second * gate_tan)
            ).astype(BF)
            terms[k, 1, rows, pl.ds(HI + start, 128)] = (down_first * gate_tan).astype(BF)
        for later in range(2):
            for side in range(2):
                ag1(k, side, later).start()

    def forward_terms(k):
        arrived(terms.at[k, :, pl.ds(0, OWN)], ag1_recv.at[0, k])
        for side in range(2):
            ag2(k, side).start()

    def pair(k, h):
        return remote(pair_out.at[k, h], pair_in.at[k, h], pair_recv.at[k, h], {"row": sib})

    def row_copy(k, h, away):
        other, where = peer(away)
        return remote(row_out.at[k, h, other], row_in.at[k, h, chip], row_recv.at[k, h], {"row": where})

    dsum[...] = jnp.zeros_like(dsum)

    def backward(k):
        arrived(terms.at[k, :, pl.ds(0, OWN)], ag1_recv.at[1, k])
        arrived(terms.at[k, :, pl.ds(0, OWN)], ag2_recv.at[k])
        slot = lax.rem(k, 2)

        @pl.loop(0, 2)
        def _(h):
            cols = pl.ds(aligned(h * FH, FH), FH)
            res[...] = lax.dot_general(
                terms[k].reshape(2 * CT, HI2), w[cols, :], NT, preferred_element_type=F32
            )
            prod = res[CT:, :] * signs[k, :, cols].astype(F32)
            dsum[:, cols] += jnp.sum(prod.reshape(CT // 8, 8, FH), axis=0)

            @pl.loop(0, CHIPS)
            def _(m):
                rows = pl.ds(aligned(2 * SUB * m, 2 * SUB), 2 * SUB)
                for keep, at in ((False, 1 - core), (True, core)):
                    first = aligned(2 * SUB * m + SUB * at, SUB)
                    both = jnp.concatenate(
                        [res[pl.ds(first, SUB), :], res[pl.ds(aligned(CT + first, SUB), SUB), :]], axis=0
                    )
                    if keep:
                        mine[slot, h, rows] = both
                    else:
                        pair_out[k, h, rows] = both.astype(BF)

            pair(k, h).start()

    def send_rows(k):
        slot = lax.rem(k, 2)

        @pl.loop(0, 2)
        def _(h):
            pair(k, h).wait_recv()

            @pl.loop(0, CHIPS)
            def _(m):
                rows = pl.ds(aligned(2 * SUB * m, 2 * SUB), 2 * SUB)
                row_out[k, h, m] = (mine[slot, h, rows] + pair_in[k, h, rows].astype(F32)).astype(BF)

            for away in ALL:
                row_copy(k, h, away).start()

            row_in[k, h, chip] = row_out[k, h, chip]

    def finish(k):
        rows = pl.ds(aligned(SUB * k, SUB), SUB)
        for h in range(2):
            arrived(row_in.at[k, h, pl.ds(0, CHIPS - 1)], row_recv.at[k, h])

            total_k = row_in[k, h, 0].astype(F32)
            for m in range(1, CHIPS):
                total_k = total_k + row_in[k, h, m].astype(F32)
            cols = pl.ds(h * FH, FH)
            total[0, rows, cols] = total_k[:SUB]
            total[1, rows, cols] = total_k[SUB:]

    def d1(away):
        return remote(dbuf1.at[chip], dbuf1.at[chip], d1_recv.at[0], {"row": peer(away)[1]})

    quad = 2 * rep + core

    def d2(which):
        where = ({"row": sib}, {"rep": 1 - rep}, {"rep": 1 - rep, "row": sib})[which]
        return remote(dbuf2.at[quad], dbuf2.at[quad], d2_recv.at[0], where)

    @pl.loop(0, NCH + 3)
    def _(s):
        @pl.when(s < NCH)
        def _():
            work_terms(s)

        @pl.when(s == 0)
        def _():
            fold(2, NCH - 1)

        @pl.when(jnp.logical_and(s >= 2, s < NCH + 2))
        def _():
            send_rows(s - 2)

        @pl.when(jnp.logical_and(s >= 1, s < NCH + 1))
        def _():
            backward(s - 1)

        @pl.when(s < NCH)
        def _():
            forward_terms(s)

        @pl.when(s == NCH)
        def _():
            dbuf1[chip] = jnp.sum(dsum[...], axis=0, keepdims=True)
            for away in ALL:
                d1(away).start()

        @pl.when(s == NCH + 1)
        def _():
            arrived(dbuf1.at[pl.ds(0, CHIPS - 1)], d1_recv.at[0])
            dbuf2[quad] = jnp.sum(dbuf1[...], axis=0)
            for which in range(3):
                d2(which).start()

        @pl.when(s >= 3)
        def _():
            finish(s - 3)

    both_out[...] = total[...].astype(BF)
    arrived(dbuf2.at[pl.ds(0, 3)], d2_recv.at[0])
    diag_out[...] = jnp.sum(dbuf2[...], axis=0) * (1.0 / (REPS * ROWS * NCH * SUB))

    for block in (in0, in1, in2, red0, red1, red2, pair_out):
        sent(block)
    sent(gathered.at[pl.ds(0, CHIPS - 1)])
    sent(gathered.at[pl.ds(0, CHIPS)])
    sent(terms.at[:, :, pl.ds(0, 2 * OWN)])
    sent(terms.at[:, :, pl.ds(0, OWN)])
    sent(row_out.at[:, :, pl.ds(0, CHIPS - 1)])
    sent(dbuf1.at[pl.ds(0, CHIPS - 1)])
    sent(dbuf2.at[pl.ds(0, 3)])


def write_out(total, diag, grad_out, hess_out, diag_out):
    grad_out[...] = total[0]
    hess_out[...] = total[1]
    diag_out[...] = diag[...]


def local(tokens, probe_bits, cot_codes, cot_scales, w_gate, w_up, w_down):
    split = (ROWS, NCH, SUB)
    vm = pl.BlockSpec(memory_space=pltpu.VMEM)
    hbm = pl.BlockSpec(memory_space=pl.ANY)
    dma = pltpu.SemaphoreType.DMA
    total, diag = pl.pallas_call(
        kernel,
        out_shape=(
            jax.ShapeDtypeStruct((2, NCH * SUB, FE), BF),
            jax.ShapeDtypeStruct((1, FE), F32),
        ),
        in_specs=[hbm] * 7,
        out_specs=[vm] * 2,
        scratch_shapes=[
            pltpu.VMEM((FE, HI2), BF),
            pltpu.VMEM((HI, FE), BF),
            pltpu.VMEM((NCH, ROWS, SUB, FE), jnp.int32),
            pltpu.VMEM((NCH, ROWS, SUB, FE), jnp.int32),
            pltpu.VMEM((FE // 32, NCH * CT), jnp.int32),
            pltpu.VMEM((FE // 32, FE), BF),
            pltpu.VMEM((NCH * CT, FE // 32), BF),
            pltpu.VMEM((NCH, CT, FE), BF),
            pltpu.VMEM((2 * CT, FE), BF),
            pltpu.VMEM((ROWS, NCH * SUB, FE), BF),
            pltpu.VMEM((NCH, CT, FE), BF),
            pltpu.VMEM((NCH, CT, HI), BF),
            pltpu.VMEM((NCH, CT, HI2), BF),
            pltpu.VMEM((NCH, CT, HI2), BF),
            pltpu.VMEM((2, NCH, HALF, HI), BF),
            pltpu.VMEM((2, NCH, HALF, HI2), BF),
            pltpu.VMEM((2, NCH, HALF, HI2), BF),
            pltpu.VMEM((2, NCH, OWN, HI), BF),
            pltpu.VMEM((2, NCH, OWN, HI2), BF),
            pltpu.VMEM((2, NCH, OWN, HI2), BF),
            pltpu.VMEM((NCH, 2, CT, HI2), BF),
            pltpu.VMEM((2, NCH * SUB, FE), F32),
            pltpu.VMEM((2, 2, CT, FH), F32),
            pltpu.VMEM((NCH, 2, CT, FH), BF),
            pltpu.VMEM((NCH, 2, CT, FH), BF),
            pltpu.VMEM((NCH, 2, CHIPS, 2 * SUB, FH), BF),
            pltpu.VMEM((NCH, 2, CHIPS, 2 * SUB, FH), BF),
            pltpu.VMEM((8, FE), F32),
            pltpu.VMEM((CHIPS, 1, FE), F32),
            pltpu.VMEM((4, 1, FE), F32),
            pltpu.VMEM((2 * CT, FH), F32),
            dma((2 * NCH + 5,)), dma((1,)),
            dma((2,)), dma((1,)),
            dma((2 * NCH + 2,)), dma((2 * NCH + 2,)),
            dma((2, NCH)), dma((NCH,)),
            dma((NCH, 2)), dma((NCH, 2)),
            dma((1,)), dma((1,)),
            pltpu.SemaphoreType.REGULAR((2,)),
        ],
        compiler_params=pltpu.CompilerParams(
            collective_id=0, has_side_effects=True, vmem_limit_bytes=63 * 2**20
        ),
    )(
        tokens,
        probe_bits.reshape(split + (FE,)),
        cot_codes.reshape(split + (FE,)),
        cot_scales.T,
        w_gate,
        w_up,
        w_down,
    )
    return pl.pallas_call(
        write_out,
        out_shape=(
            jax.ShapeDtypeStruct((NCH * SUB, FE), BF),
            jax.ShapeDtypeStruct((NCH * SUB, FE), BF),
            jax.ShapeDtypeStruct((FE,), F32),
        ),
        in_specs=[vm] * 2,
        out_specs=[vm] * 3,
    )(total, diag.reshape(FE))


def solution(mesh):
    in_specs = (
        P(("rep", "row"), "col"),
        P("rep", "col"),
        P("rep", "col"),
        P("rep", "col"),
        P("col", "row"),
        P("col", "row"),
        P("row", "col"),
    )
    out_specs = (P(("rep", "row"), "col"), P(("rep", "row"), "col"), P("col"))
    return jax.shard_map(local, mesh=mesh, in_specs=in_specs, out_specs=out_specs, check_vma=False)
```

```python
import functools

import jax
import jax.numpy as jnp
from jax import lax
from jax.experimental import pallas as pl
from jax.experimental.pallas import tpu as pltpu
from jax.sharding import PartitionSpec as P

MESH = pl.DeviceIdType.MESH
BF = jnp.bfloat16
F32 = jnp.float32
REPS, ROWS, COLS = 2, 16, 4
CHIPS = ROWS // 2
ZS = CHIPS // 2
NEAR = ((1, 0), (3, 0))
MID = ((2, 0), (0, 1))
FAR = ((1, 1), (3, 1), (2, 1))
ALL = FAR[::-1] + MID + NEAR
NCH = 4
SUB = 8
CT = ROWS * SUB
OWN = CT // COLS
HALF = OWN // 2
FE = 2048
HI = 896
HI2 = 2 * HI
FH = FE // 2
NT = (((1,), (1,)), ((), ()))


def aligned(value, step):
    return pl.multiple_of(value, step)


def kernel(
    tok, bits_hbm, codes_hbm, scales_hbm, wg_hbm, wu_hbm, wd_hbm,
    both_out, diag_out,
    w, wd, bits, codes, scales, spread, power, signs, cot, gathered, ordered,
    part0, part1, part2, in0, in1, in2, red0, red1, red2, terms, total, mine,
    pair_out, pair_in, row_out, row_in, dsum, dbuf1, dbuf2, res,
    load_sem, send_sem, tok_recv, sib_recv, rs1_recv, rs2_recv, ag1_recv, ag2_recv,
    pair_recv, row_recv, d1_recv, d2_recv, ready,
):
    rep = lax.axis_index("rep")
    row = lax.axis_index("row")
    col = lax.axis_index("col")
    core = lax.rem(row, 2)
    chip = row // 2
    sib = row + 1 - 2 * core
    left = lax.rem(col + COLS - 1, COLS)
    right = lax.rem(col + 1, COLS)
    opp = lax.rem(col + 2, COLS)
    sides = (left, right)

    z, xh = chip // 2, lax.rem(chip, 2)

    def peer(away):
        other = lax.rem(z + away[0], ZS) * 2 + lax.rem(xh + away[1], 2)
        return other, 2 * other + core

    def load_bits(k):
        return pltpu.make_async_copy(bits_hbm.at[:, k], bits.at[k], load_sem.at[k])

    def load_codes(k):
        return pltpu.make_async_copy(codes_hbm.at[:, k], codes.at[k], load_sem.at[NCH + k])

    load_wg = pltpu.make_async_copy(wg_hbm, w.at[:, pl.ds(0, HI)], load_sem.at[2 * NCH])
    load_wu = pltpu.make_async_copy(wu_hbm, w.at[:, pl.ds(HI, HI)], load_sem.at[2 * NCH + 1])
    load_wd = pltpu.make_async_copy(wd_hbm, wd, load_sem.at[2 * NCH + 2])
    load_sc = pltpu.make_async_copy(scales_hbm, scales, load_sem.at[2 * NCH + 3])
    load_tok = pltpu.make_async_copy(tok, gathered.at[row], load_sem.at[2 * NCH + 4])
    load_sc.start()
    load_codes(0).start()
    load_codes(1).start()
    load_tok.start()
    load_wd.start()
    load_codes(2).start()
    load_codes(3).start()
    load_bits(0).start()
    load_wg.start()
    load_wu.start()
    for k in range(1, NCH):
        load_bits(k).start()

    barrier = pltpu.get_barrier_semaphore()

    def tell(sem, where):
        pl.semaphore_signal(sem, inc=1, device_id=where, device_id_type=MESH)

    opposite_row = peer((0, 1))[1]
    for side in sides:
        tell(barrier, {"col": side})
    tell(barrier, {"row": sib})
    for away in NEAR:
        tell(barrier, {"row": peer(away)[1]})
    opposite_sib = opposite_row + 1 - 2 * core
    for other_row in (row, sib, opposite_row, opposite_sib):
        tell(barrier, {"rep": 1 - rep, "row": other_row})

    def enter_first():
        pl.semaphore_wait(barrier, 9)
        for away in NEAR:
            tell(ready.at[0], {"row": peer(away)[1]})
        tell(ready.at[0], {"rep": 1 - rep})

    def enter_second():
        pl.semaphore_wait(ready.at[0], 3)
        tell(ready.at[1], {"row": opposite_row})

    def enter_third():
        pl.semaphore_wait(ready.at[1], 1)

    def remote(src, dst, recv, where):
        return pltpu.make_async_remote_copy(
            src_ref=src, dst_ref=dst, send_sem=send_sem.at[0], recv_sem=recv, device_id=where, device_id_type=MESH
        )

    def arrived(block, recv):
        remote(block, block, recv, {"row": sib}).wait_recv()

    def sent(block):
        remote(block, block, sib_recv.at[0], {"row": sib}).wait_send()

    across = (0, 1)
    column = NEAR + ((2, 0),)

    def tok_rows(h):
        return pl.ds(2 * SUB * h, 2 * SUB)

    def send_tok(block_row, h, where, recv):
        block = gathered.at[block_row, tok_rows(h)]
        return remote(block, block, recv, {"row": where})

    def own_tok(away, h):
        return send_tok(row, h, peer(away)[1], tok_recv.at[0 if away == across else 1, h])

    def onward_tok(away, h):
        return send_tok(opposite_row, h, peer(away)[1], tok_recv.at[1, h])

    def share_tok(block_row, h):
        return send_tok(block_row, h, sib, sib_recv.at[h])

    lanes = lax.broadcasted_iota(jnp.int32, spread.shape, 1) // 32
    spread[...] = (lanes == lax.broadcasted_iota(jnp.int32, spread.shape, 0)).astype(F32).astype(BF)
    at = lax.broadcasted_iota(jnp.int32, (NCH * CT, NCH * CT), 0)
    token = (at % CT) // SUB * (NCH * SUB) + at // CT * SUB + at % SUB
    pick = (token == lax.broadcasted_iota(jnp.int32, (NCH * CT, NCH * CT), 1)).astype(F32).astype(BF)
    load_sc.wait()
    raised = (lax.shift_left(1, scales[...] + 2).astype(F32) * 2.0**-7).astype(BF)
    power[...] = lax.dot_general(pick, raised, NT, preferred_element_type=F32).astype(BF)

    batches = ((part0, in0, red0, 2, 0), (part1, in1, red1, 1, 2), (part2, in2, red2, 1, 2 + NCH))

    def rs1(batch, k, side):
        part, inn, _, n, base = batches[batch]
        ks = pl.ds(k * n, n)
        src = part.at[ks, pl.ds(aligned(OWN * opp + HALF * side, HALF), HALF)]
        return remote(src, inn.at[side, ks], rs1_recv.at[base + k], {"col": sides[side]})

    def rs2(batch, k, side):
        part, _, red, n, base = batches[batch]
        ks = pl.ds(k * n, n)
        src = part.at[ks, pl.ds(aligned(OWN * sides[side], OWN), OWN)]
        return remote(src, red.at[side, ks], rs2_recv.at[base + k], {"col": sides[side]})

    def start_rs1(batch, k):
        for side in range(2):
            rs1(batch, k, side).start()

    def fold(batch, k):
        part, inn, _, n, base = batches[batch]
        arrived(inn.at[:, pl.ds(k * n, n)], rs1_recv.at[base + k])
        for side in range(2):
            rows = pl.ds(aligned(OWN * sides[side] + HALF * side, HALF), HALF)
            for i in range(n):
                at = k * n + i
                part[at, rows] = (part[at, rows].astype(F32) + inn[side, at].astype(F32)).astype(BF)
            rs2(batch, k, side).start()

    def folded(batch, k):
        _, _, red, n, base = batches[batch]
        arrived(red.at[:, pl.ds(k * n, n)], rs2_recv.at[base + k])

    def down(p):
        for i in range(2):
            load_codes(2 * p + i).wait()

        @pl.loop(0, FE // 512)
        def _(n):
            cols = pl.ds(aligned(n * 512, 512), 512)
            code = codes[pl.ds(2 * p, 2), :, :, cols].reshape(2 * CT, 512)
            size = lax.shift_left((code & 7) | 8, ((code >> 3) & 15) - 5)
            value = jnp.where(code >= 128, -size, size).astype(F32)
            wide = jnp.dot(
                power[pl.ds(aligned(2 * CT * p, 2 * CT), 2 * CT), :], spread[:, cols], preferred_element_type=F32
            )
            cot[:, cols] = (value * wide).astype(BF)

        if p == 0:
            load_wd.wait()

        part0[pl.ds(2 * p, 2)] = (
            lax.dot_general(cot[...], wd[...], NT, preferred_element_type=F32).astype(BF).reshape(2, CT, HI)
        )

    def tangent(k):
        load_bits(k).wait()
        signs[k] = (2 * bits[k].reshape(CT, FE) - 1).astype(F32).astype(BF)

        @pl.when(k == 0)
        def _():
            load_wg.wait()
            load_wu.wait()

        part1[k] = jnp.dot(signs[k], w[...], preferred_element_type=F32).astype(BF)
        start_rs1(1, k)

    def primal(k):
        part2[k] = jnp.dot(ordered[k], w[...], preferred_element_type=F32).astype(BF)
        start_rs1(2, k)

    def onward_tokens(h):
        arrived(gathered.at[opposite_row, tok_rows(h)], tok_recv.at[0, h])
        for away in column:
            onward_tok(away, h).start()
        share_tok(opposite_row, h).start()

    def gather_tokens(h):
        arrived(gathered.at[pl.ds(0, 6), tok_rows(h)], tok_recv.at[1, h])
        for away in column:
            other, where = peer(away)
            share_tok(where, h).start()
            share_tok(peer((away[0], 1))[1], h).start()

    def order_tokens(h):
        arrived(gathered.at[pl.ds(0, CHIPS), tok_rows(h)], sib_recv.at[h])

        @pl.loop(0, CHIPS)
        def _(q):
            even = gathered[2 * q, tok_rows(h)].astype(F32)
            odd = gathered[2 * q + 1, tok_rows(h)].astype(F32)
            out = pl.ds(aligned(2 * SUB * q, 2 * SUB), 2 * SUB)
            ordered[2 * h, out] = jnp.concatenate([even[:SUB], odd[:SUB]], axis=0).astype(BF)
            ordered[2 * h + 1, out] = jnp.concatenate([even[SUB:], odd[SUB:]], axis=0).astype(BF)

    down(0)
    enter_first()
    start_rs1(0, 0)
    load_tok.wait()
    for away in NEAR:
        own_tok(away, 0).start()
    share_tok(row, 0).start()
    down(1)
    start_rs1(0, 1)
    enter_second()
    own_tok(across, 0).start()
    own_tok((2, 0), 0).start()

    @pl.loop(0, NCH)
    def _(s):
        tangent(s)

        @pl.when(s == 0)
        def _():
            fold(0, 0)
            fold(0, 1)

        @pl.when(s == 1)
        def _():
            onward_tokens(0)
            for away in (across,) + column:
                own_tok(away, 1).start()
            share_tok(row, 1).start()

        @pl.when(s == 3)
        def _():
            gather_tokens(0)
            onward_tokens(1)

        @pl.when(s >= 2)
        def _():
            fold(1, s - 2)

    order_tokens(0)

    @pl.loop(0, NCH)
    def _(s):
        @pl.when(s == 2)
        def _():
            order_tokens(1)

        primal(s)

        @pl.when(s == 0)
        def _():
            enter_third()

        @pl.when(s == 1)
        def _():
            gather_tokens(1)

        @pl.when(s < 2)
        def _():
            fold(1, s + 2)

        @pl.when(s >= 2)
        def _():
            fold(2, s - 2)

    fold(2, 2)

    def ag1(k, side, later):
        half = 1 - side if later else side
        block = terms.at[k, :, pl.ds(aligned(OWN * col + HALF * half, HALF), HALF)]
        return remote(block, block, ag1_recv.at[later, k], {"col": sides[side]})

    def ag2(k, side):
        rows = pl.ds(aligned(OWN * sides[1 - side] + HALF * side, HALF), HALF)
        block = terms.at[k, :, rows]
        return remote(block, block, ag2_recv.at[k], {"col": sides[side]})

    def work_terms(k):
        folded(1, k)
        folded(2, k)

        @pl.when(lax.rem(k, 2) == 0)
        def _():
            folded(0, k // 2)

        rows = pl.ds(aligned(OWN * col, OWN), OWN)

        def full(part, red, start):
            cols = pl.ds(start, 128)
            return part[k, rows, cols].astype(F32) + red[0, k, :, cols].astype(F32) + red[1, k, :, cols].astype(F32)

        for start in range(0, HI, 128):
            gate_tan = full(part1, red1, start)
            up_tan = full(part1, red1, HI + start)
            down_back = full(part0, red0, start)
            gate_pre = full(part2, red2, start)
            up_pre = full(part2, red2, HI + start)
            sig = 1.0 / (1.0 + jnp.exp(-gate_pre))
            rest = 1.0 - sig
            first = sig * (1.0 + gate_pre * rest)
            second = sig * rest * (2.0 + gate_pre * (1.0 - 2.0 * sig))
            down_first = down_back * first
            terms[k, 0, rows, pl.ds(start, 128)] = (down_first * up_pre).astype(BF)
            terms[k, 0, rows, pl.ds(HI + start, 128)] = (down_back * gate_pre * sig).astype(BF)
            terms[k, 1, rows, pl.ds(start, 128)] = (
                down_back * (up_tan * first + up_pre * second * gate_tan)
            ).astype(BF)
            terms[k, 1, rows, pl.ds(HI + start, 128)] = (down_first * gate_tan).astype(BF)
        for later in range(2):
            for side in range(2):
                ag1(k, side, later).start()

    def forward_terms(k):
        arrived(terms.at[k, :, pl.ds(0, OWN)], ag1_recv.at[0, k])
        for side in range(2):
            ag2(k, side).start()

    def pair(k, h):
        return remote(pair_out.at[k, h], pair_in.at[k, h], pair_recv.at[k, h], {"row": sib})

    def row_copy(k, h, away):
        other, where = peer(away)
        return remote(row_out.at[k, h, other], row_in.at[k, h, chip], row_recv.at[k, h], {"row": where})

    dsum[...] = jnp.zeros_like(dsum)

    def backward(k):
        arrived(terms.at[k, :, pl.ds(0, OWN)], ag1_recv.at[1, k])
        arrived(terms.at[k, :, pl.ds(0, OWN)], ag2_recv.at[k])
        slot = lax.rem(k, 2)

        @pl.loop(0, 2)
        def _(h):
            cols = pl.ds(aligned(h * FH, FH), FH)
            res[...] = lax.dot_general(
                terms[k].reshape(2 * CT, HI2), w[cols, :], NT, preferred_element_type=F32
            )
            prod = res[CT:, :] * signs[k, :, cols].astype(F32)
            dsum[:, cols] += jnp.sum(prod.reshape(CT // 8, 8, FH), axis=0)

            @pl.loop(0, CHIPS)
            def _(m):
                rows = pl.ds(aligned(2 * SUB * m, 2 * SUB), 2 * SUB)
                for keep, at in ((False, 1 - core), (True, core)):
                    first = aligned(2 * SUB * m + SUB * at, SUB)
                    both = jnp.concatenate(
                        [res[pl.ds(first, SUB), :], res[pl.ds(aligned(CT + first, SUB), SUB), :]], axis=0
                    )
                    if keep:
                        mine[slot, h, rows] = both
                    else:
                        pair_out[k, h, rows] = both.astype(BF)

            pair(k, h).start()

    def send_rows(k):
        slot = lax.rem(k, 2)

        @pl.loop(0, 2)
        def _(h):
            pair(k, h).wait_recv()

            @pl.loop(0, CHIPS)
            def _(m):
                rows = pl.ds(aligned(2 * SUB * m, 2 * SUB), 2 * SUB)
                row_out[k, h, m] = (mine[slot, h, rows] + pair_in[k, h, rows].astype(F32)).astype(BF)

            for away in ALL:
                row_copy(k, h, away).start()

            row_in[k, h, chip] = row_out[k, h, chip]

    def finish(k):
        rows = pl.ds(aligned(SUB * k, SUB), SUB)
        for h in range(2):
            arrived(row_in.at[k, h, pl.ds(0, CHIPS - 1)], row_recv.at[k, h])

            total_k = row_in[k, h, 0].astype(F32)
            for m in range(1, CHIPS):
                total_k = total_k + row_in[k, h, m].astype(F32)
            cols = pl.ds(h * FH, FH)
            total[0, rows, cols] = total_k[:SUB]
            total[1, rows, cols] = total_k[SUB:]

    def d1(away):
        return remote(dbuf1.at[z], dbuf1.at[z], d1_recv.at[0], {"row": peer(away)[1]})

    octet = 4 * rep + 2 * xh + core

    def d2():
        block = dbuf2.at[octet]
        for other_row in (opposite_row, opposite_sib):
            yield remote(block, block, d2_recv.at[0], {"row": other_row})
        for other_row in (row, sib, opposite_row, opposite_sib):
            yield remote(block, block, d2_recv.at[0], {"rep": 1 - rep, "row": other_row})
        yield remote(block, block, d2_recv.at[0], {"row": sib})

    @pl.loop(0, NCH + 3)
    def _(s):
        @pl.when(s < NCH)
        def _():
            work_terms(s)

        @pl.when(s == 0)
        def _():
            fold(2, NCH - 1)

        @pl.when(jnp.logical_and(s >= 2, s < NCH + 2))
        def _():
            send_rows(s - 2)

        @pl.when(jnp.logical_and(s >= 1, s < NCH + 1))
        def _():
            backward(s - 1)

        @pl.when(s < NCH)
        def _():
            forward_terms(s)

        @pl.when(s == NCH)
        def _():
            dbuf1[z] = jnp.sum(dsum[...], axis=0, keepdims=True)
            for away in column[::-1]:
                d1(away).start()

        @pl.when(s == NCH + 1)
        def _():
            arrived(dbuf1.at[pl.ds(0, ZS - 1)], d1_recv.at[0])
            dbuf2[octet] = jnp.sum(dbuf1[...], axis=0)
            for copy in d2():
                copy.start()

        @pl.when(s >= 3)
        def _():
            finish(s - 3)

    both_out[...] = total[...].astype(BF)
    arrived(dbuf2.at[pl.ds(0, 7)], d2_recv.at[0])
    diag_out[...] = jnp.sum(dbuf2[...], axis=0) * (1.0 / (REPS * ROWS * NCH * SUB))

    for block in (in0, in1, in2, red0, red1, red2, pair_out):
        sent(block)
    sent(gathered.at[pl.ds(0, CHIPS - 1)])
    sent(gathered.at[pl.ds(0, CHIPS)])
    sent(terms.at[:, :, pl.ds(0, 2 * OWN)])
    sent(terms.at[:, :, pl.ds(0, OWN)])
    sent(row_out.at[:, :, pl.ds(0, CHIPS - 1)])
    sent(dbuf1.at[pl.ds(0, ZS - 1)])
    sent(dbuf2.at[pl.ds(0, 7)])


def write_out(total, diag, grad_out, hess_out, diag_out):
    grad_out[...] = total[0]
    hess_out[...] = total[1]
    diag_out[...] = diag[...]


def local(tokens, probe_bits, cot_codes, cot_scales, w_gate, w_up, w_down):
    split = (ROWS, NCH, SUB)
    vm = pl.BlockSpec(memory_space=pltpu.VMEM)
    hbm = pl.BlockSpec(memory_space=pl.ANY)
    dma = pltpu.SemaphoreType.DMA
    total, diag = pl.pallas_call(
        kernel,
        out_shape=(
            jax.ShapeDtypeStruct((2, NCH * SUB, FE), BF),
            jax.ShapeDtypeStruct((1, FE), F32),
        ),
        in_specs=[hbm] * 7,
        out_specs=[vm] * 2,
        scratch_shapes=[
            pltpu.VMEM((FE, HI2), BF),
            pltpu.VMEM((HI, FE), BF),
            pltpu.VMEM((NCH, ROWS, SUB, FE), jnp.int32),
            pltpu.VMEM((NCH, ROWS, SUB, FE), jnp.int32),
            pltpu.VMEM((FE // 32, NCH * CT), jnp.int32),
            pltpu.VMEM((FE // 32, FE), BF),
            pltpu.VMEM((NCH * CT, FE // 32), BF),
            pltpu.VMEM((NCH, CT, FE), BF),
            pltpu.VMEM((2 * CT, FE), BF),
            pltpu.VMEM((ROWS, NCH * SUB, FE), BF),
            pltpu.VMEM((NCH, CT, FE), BF),
            pltpu.VMEM((NCH, CT, HI), BF),
            pltpu.VMEM((NCH, CT, HI2), BF),
            pltpu.VMEM((NCH, CT, HI2), BF),
            pltpu.VMEM((2, NCH, HALF, HI), BF),
            pltpu.VMEM((2, NCH, HALF, HI2), BF),
            pltpu.VMEM((2, NCH, HALF, HI2), BF),
            pltpu.VMEM((2, NCH, OWN, HI), BF),
            pltpu.VMEM((2, NCH, OWN, HI2), BF),
            pltpu.VMEM((2, NCH, OWN, HI2), BF),
            pltpu.VMEM((NCH, 2, CT, HI2), BF),
            pltpu.VMEM((2, NCH * SUB, FE), F32),
            pltpu.VMEM((2, 2, CT, FH), F32),
            pltpu.VMEM((NCH, 2, CT, FH), BF),
            pltpu.VMEM((NCH, 2, CT, FH), BF),
            pltpu.VMEM((NCH, 2, CHIPS, 2 * SUB, FH), BF),
            pltpu.VMEM((NCH, 2, CHIPS, 2 * SUB, FH), BF),
            pltpu.VMEM((8, FE), F32),
            pltpu.VMEM((ZS, 1, FE), F32),
            pltpu.VMEM((8, 1, FE), F32),
            pltpu.VMEM((2 * CT, FH), F32),
            dma((2 * NCH + 5,)), dma((1,)),
            dma((2, 2)), dma((2,)),
            dma((2 * NCH + 2,)), dma((2 * NCH + 2,)),
            dma((2, NCH)), dma((NCH,)),
            dma((NCH, 2)), dma((NCH, 2)),
            dma((1,)), dma((1,)),
            pltpu.SemaphoreType.REGULAR((2,)),
        ],
        compiler_params=pltpu.CompilerParams(
            collective_id=0, has_side_effects=True, vmem_limit_bytes=63 * 2**20
        ),
    )(
        tokens,
        probe_bits.reshape(split + (FE,)),
        cot_codes.reshape(split + (FE,)),
        cot_scales.T,
        w_gate,
        w_up,
        w_down,
    )
    return pl.pallas_call(
        write_out,
        out_shape=(
            jax.ShapeDtypeStruct((NCH * SUB, FE), BF),
            jax.ShapeDtypeStruct((NCH * SUB, FE), BF),
            jax.ShapeDtypeStruct((FE,), F32),
        ),
        in_specs=[vm] * 2,
        out_specs=[vm] * 3,
    )(total, diag.reshape(FE))


def solution(mesh):
    in_specs = (
        P(("rep", "row"), "col"),
        P("rep", "col"),
        P("rep", "col"),
        P("rep", "col"),
        P("col", "row"),
        P("col", "row"),
        P("row", "col"),
    )
    out_specs = (P(("rep", "row"), "col"), P(("rep", "row"), "col"), P("col"))
    return jax.shard_map(local, mesh=mesh, in_specs=in_specs, out_specs=out_specs, check_vma=False)
```

```python
import functools

import jax
import jax.numpy as jnp
from jax import lax
from jax.experimental import pallas as pl
from jax.experimental.pallas import tpu as pltpu
from jax.sharding import PartitionSpec as P

MESH = pl.DeviceIdType.MESH
BF = jnp.bfloat16
F32 = jnp.float32
REPS, ROWS, COLS = 2, 16, 4
CHIPS = ROWS // 2
ZS = CHIPS // 2
NEAR = ((1, 0), (3, 0))
MID = ((2, 0), (0, 1))
FAR = ((1, 1), (3, 1), (2, 1))
ALL = FAR[::-1] + MID + NEAR
NCH = 4
SUB = 8
CT = ROWS * SUB
OWN = CT // COLS
HALF = OWN // 2
FE = 2048
HI = 896
HI2 = 2 * HI
FH = FE // 2
NT = (((1,), (1,)), ((), ()))


def aligned(value, step):
    return pl.multiple_of(value, step)


def kernel(
    tok, bits_hbm, codes_hbm, scales_hbm, wg_hbm, wu_hbm, wd_hbm,
    both_out, diag_out,
    w, wd, bits, codes, scales, spread, power, signs, cot, gathered, ordered,
    part0, part1, part2, in0, in1, in2, red0, red1, red2, terms, total, mine,
    pair_out, pair_in, row_out, row_in, dsum, dbuf1, dbuf2, res,
    load_sem, send_sem, tok_recv, sib_recv, rs1_recv, rs2_recv, ag1_recv, ag2_recv,
    pair_recv, row_recv, d1_recv, d2_recv, ready,
):
    rep = lax.axis_index("rep")
    row = lax.axis_index("row")
    col = lax.axis_index("col")
    core = lax.rem(row, 2)
    chip = row // 2
    sib = row + 1 - 2 * core
    left = lax.rem(col + COLS - 1, COLS)
    right = lax.rem(col + 1, COLS)
    opp = lax.rem(col + 2, COLS)
    sides = (left, right)

    z, xh = chip // 2, lax.rem(chip, 2)

    def peer(away):
        other = lax.rem(z + away[0], ZS) * 2 + lax.rem(xh + away[1], 2)
        return other, 2 * other + core

    def load_bits(k):
        return pltpu.make_async_copy(bits_hbm.at[:, k], bits.at[k], load_sem.at[k])

    def load_codes(k):
        return pltpu.make_async_copy(codes_hbm.at[:, k], codes.at[k], load_sem.at[NCH + k])

    load_wg = pltpu.make_async_copy(wg_hbm, w.at[:, pl.ds(0, HI)], load_sem.at[2 * NCH])
    load_wu = pltpu.make_async_copy(wu_hbm, w.at[:, pl.ds(HI, HI)], load_sem.at[2 * NCH + 1])
    load_wd = pltpu.make_async_copy(wd_hbm, wd, load_sem.at[2 * NCH + 2])
    load_sc = pltpu.make_async_copy(scales_hbm, scales, load_sem.at[2 * NCH + 3])
    load_tok = pltpu.make_async_copy(tok, gathered.at[row], load_sem.at[2 * NCH + 4])
    load_sc.start()
    load_codes(0).start()
    load_codes(1).start()
    load_tok.start()
    load_wd.start()
    load_codes(2).start()
    load_codes(3).start()
    load_bits(0).start()
    load_wg.start()
    load_wu.start()
    for k in range(1, NCH):
        load_bits(k).start()

    barrier = pltpu.get_barrier_semaphore()

    def tell(sem, where):
        pl.semaphore_signal(sem, inc=1, device_id=where, device_id_type=MESH)

    opposite_row = peer((0, 1))[1]
    for side in sides:
        tell(barrier, {"col": side})
    tell(barrier, {"row": sib})
    for away in NEAR:
        tell(barrier, {"row": peer(away)[1]})
    for other_row in (row, sib, opposite_row):
        tell(barrier, {"rep": 1 - rep, "row": other_row})

    def enter_first():
        pl.semaphore_wait(barrier, 8)
        for away in NEAR:
            tell(ready.at[0], {"row": peer(away)[1]})
        tell(ready.at[0], {"rep": 1 - rep})

    def enter_second():
        pl.semaphore_wait(ready.at[0], 3)
        tell(ready.at[1], {"row": opposite_row})

    def enter_third():
        pl.semaphore_wait(ready.at[1], 1)

    def remote(src, dst, recv, where):
        return pltpu.make_async_remote_copy(
            src_ref=src, dst_ref=dst, send_sem=send_sem.at[0], recv_sem=recv, device_id=where, device_id_type=MESH
        )

    def arrived(block, recv):
        remote(block, block, recv, {"row": sib}).wait_recv()

    def sent(block):
        remote(block, block, tok_recv.at[0], {"row": sib}).wait_send()

    across = (0, 1)
    column = NEAR + ((2, 0),)

    def send_tok(block_row, where, recv):
        block = gathered.at[block_row]
        return remote(block, block, recv, {"row": where})

    def own_tok(away):
        return send_tok(row, peer(away)[1], tok_recv.at[0 if away == across else 1])

    def onward_tok(away):
        return send_tok(opposite_row, peer(away)[1], tok_recv.at[1])

    def share_tok(block_row):
        return send_tok(block_row, sib, sib_recv.at[0])

    lanes = lax.broadcasted_iota(jnp.int32, spread.shape, 1) // 32
    spread[...] = (lanes == lax.broadcasted_iota(jnp.int32, spread.shape, 0)).astype(F32).astype(BF)
    at = lax.broadcasted_iota(jnp.int32, (NCH * CT, NCH * CT), 0)
    token = (at % CT) // SUB * (NCH * SUB) + at // CT * SUB + at % SUB
    pick = (token == lax.broadcasted_iota(jnp.int32, (NCH * CT, NCH * CT), 1)).astype(F32).astype(BF)
    load_sc.wait()
    raised = (lax.shift_left(1, scales[...] + 2).astype(F32) * 2.0**-7).astype(BF)
    power[...] = lax.dot_general(pick, raised, NT, preferred_element_type=F32).astype(BF)

    batches = ((part0, in0, red0, 2, 0), (part1, in1, red1, 1, 2), (part2, in2, red2, 1, 2 + NCH))

    def rs1(batch, k, side):
        part, inn, _, n, base = batches[batch]
        ks = pl.ds(k * n, n)
        src = part.at[ks, pl.ds(aligned(OWN * opp + HALF * side, HALF), HALF)]
        return remote(src, inn.at[side, ks], rs1_recv.at[base + k], {"col": sides[side]})

    def rs2(batch, k, side):
        part, _, red, n, base = batches[batch]
        ks = pl.ds(k * n, n)
        src = part.at[ks, pl.ds(aligned(OWN * sides[side], OWN), OWN)]
        return remote(src, red.at[side, ks], rs2_recv.at[base + k], {"col": sides[side]})

    def start_rs1(batch, k):
        for side in range(2):
            rs1(batch, k, side).start()

    def fold(batch, k):
        part, inn, _, n, base = batches[batch]
        arrived(inn.at[:, pl.ds(k * n, n)], rs1_recv.at[base + k])
        for side in range(2):
            rows = pl.ds(aligned(OWN * sides[side] + HALF * side, HALF), HALF)
            for i in range(n):
                at = k * n + i
                part[at, rows] = (part[at, rows].astype(F32) + inn[side, at].astype(F32)).astype(BF)
            rs2(batch, k, side).start()

    def folded(batch, k):
        _, _, red, n, base = batches[batch]
        arrived(red.at[:, pl.ds(k * n, n)], rs2_recv.at[base + k])

    def down(p):
        for i in range(2):
            load_codes(2 * p + i).wait()

        @pl.loop(0, FE // 512)
        def _(n):
            cols = pl.ds(aligned(n * 512, 512), 512)
            code = codes[pl.ds(2 * p, 2), :, :, cols].reshape(2 * CT, 512)
            size = lax.shift_left((code & 7) | 8, ((code >> 3) & 15) - 5)
            value = jnp.where(code >= 128, -size, size).astype(F32)
            wide = jnp.dot(
                power[pl.ds(aligned(2 * CT * p, 2 * CT), 2 * CT), :], spread[:, cols], preferred_element_type=F32
            )
            cot[:, cols] = (value * wide).astype(BF)

        if p == 0:
            load_wd.wait()

        part0[pl.ds(2 * p, 2)] = (
            lax.dot_general(cot[...], wd[...], NT, preferred_element_type=F32).astype(BF).reshape(2, CT, HI)
        )

    def tangent(k):
        load_bits(k).wait()
        signs[k] = (2 * bits[k].reshape(CT, FE) - 1).astype(F32).astype(BF)

        @pl.when(k == 0)
        def _():
            load_wg.wait()
            load_wu.wait()

        part1[k] = jnp.dot(signs[k], w[...], preferred_element_type=F32).astype(BF)
        start_rs1(1, k)

    def primal(k):
        part2[k] = jnp.dot(ordered[k], w[...], preferred_element_type=F32).astype(BF)
        start_rs1(2, k)

    def onward_tokens():
        arrived(gathered.at[opposite_row], tok_recv.at[0])
        for away in column:
            onward_tok(away).start()
        share_tok(opposite_row).start()

    def gather_tokens():
        arrived(gathered.at[pl.ds(0, 6)], tok_recv.at[1])
        for away in column:
            other, where = peer(away)
            share_tok(where).start()
            share_tok(peer((away[0], 1))[1]).start()

    def order_tokens():
        arrived(gathered.at[pl.ds(0, CHIPS)], sib_recv.at[0])

        @pl.loop(0, CHIPS)
        def _(q):
            for h in range(NCH // 2):
                rows = pl.ds(2 * SUB * h, 2 * SUB)
                even = gathered[2 * q, rows].astype(F32)
                odd = gathered[2 * q + 1, rows].astype(F32)
                out = pl.ds(aligned(2 * SUB * q, 2 * SUB), 2 * SUB)
                ordered[2 * h, out] = jnp.concatenate([even[:SUB], odd[:SUB]], axis=0).astype(BF)
                ordered[2 * h + 1, out] = jnp.concatenate([even[SUB:], odd[SUB:]], axis=0).astype(BF)

    down(0)
    enter_first()
    start_rs1(0, 0)
    load_tok.wait()
    for away in NEAR:
        own_tok(away).start()
    share_tok(row).start()
    down(1)
    start_rs1(0, 1)
    enter_second()
    own_tok(across).start()
    own_tok((2, 0)).start()

    @pl.loop(0, NCH)
    def _(s):
        tangent(s)

        @pl.when(s == 0)
        def _():
            fold(0, 0)
            fold(0, 1)

        @pl.when(s == 1)
        def _():
            onward_tokens()

        @pl.when(s >= 2)
        def _():
            fold(1, s - 2)

    gather_tokens()
    order_tokens()
    enter_third()

    @pl.loop(0, NCH)
    def _(s):
        primal(s)

        @pl.when(s < 2)
        def _():
            fold(1, s + 2)

        @pl.when(s >= 2)
        def _():
            fold(2, s - 2)

    fold(2, 2)

    def ag1(k, side, later):
        half = 1 - side if later else side
        block = terms.at[k, :, pl.ds(aligned(OWN * col + HALF * half, HALF), HALF)]
        return remote(block, block, ag1_recv.at[later, k], {"col": sides[side]})

    def ag2(k, side):
        rows = pl.ds(aligned(OWN * sides[1 - side] + HALF * side, HALF), HALF)
        block = terms.at[k, :, rows]
        return remote(block, block, ag2_recv.at[k], {"col": sides[side]})

    def work_terms(k):
        folded(1, k)
        folded(2, k)

        @pl.when(lax.rem(k, 2) == 0)
        def _():
            folded(0, k // 2)

        rows = pl.ds(aligned(OWN * col, OWN), OWN)

        def full(part, red, start):
            cols = pl.ds(start, 128)
            return part[k, rows, cols].astype(F32) + red[0, k, :, cols].astype(F32) + red[1, k, :, cols].astype(F32)

        for start in range(0, HI, 128):
            gate_tan = full(part1, red1, start)
            up_tan = full(part1, red1, HI + start)
            down_back = full(part0, red0, start)
            gate_pre = full(part2, red2, start)
            up_pre = full(part2, red2, HI + start)
            sig = 1.0 / (1.0 + jnp.exp(-gate_pre))
            rest = 1.0 - sig
            first = sig * (1.0 + gate_pre * rest)
            second = sig * rest * (2.0 + gate_pre * (1.0 - 2.0 * sig))
            down_first = down_back * first
            terms[k, 0, rows, pl.ds(start, 128)] = (down_first * up_pre).astype(BF)
            terms[k, 0, rows, pl.ds(HI + start, 128)] = (down_back * gate_pre * sig).astype(BF)
            terms[k, 1, rows, pl.ds(start, 128)] = (
                down_back * (up_tan * first + up_pre * second * gate_tan)
            ).astype(BF)
            terms[k, 1, rows, pl.ds(HI + start, 128)] = (down_first * gate_tan).astype(BF)
        for later in range(2):
            for side in range(2):
                ag1(k, side, later).start()

    def forward_terms(k):
        arrived(terms.at[k, :, pl.ds(0, OWN)], ag1_recv.at[0, k])
        for side in range(2):
            ag2(k, side).start()

    def pair(k, h):
        return remote(pair_out.at[k, h], pair_in.at[k, h], pair_recv.at[k, h], {"row": sib})

    def row_copy(k, h, away):
        other, where = peer(away)
        return remote(row_out.at[k, h, other], row_in.at[k, h, chip], row_recv.at[k, h], {"row": where})

    dsum[...] = jnp.zeros_like(dsum)

    def backward(k):
        arrived(terms.at[k, :, pl.ds(0, OWN)], ag1_recv.at[1, k])
        arrived(terms.at[k, :, pl.ds(0, OWN)], ag2_recv.at[k])
        slot = lax.rem(k, 2)

        @pl.loop(0, 2)
        def _(h):
            cols = pl.ds(aligned(h * FH, FH), FH)
            res[...] = lax.dot_general(
                terms[k].reshape(2 * CT, HI2), w[cols, :], NT, preferred_element_type=F32
            )
            prod = res[CT:, :] * signs[k, :, cols].astype(F32)
            dsum[:, cols] += jnp.sum(prod.reshape(CT // 8, 8, FH), axis=0)

            @pl.loop(0, CHIPS)
            def _(m):
                rows = pl.ds(aligned(2 * SUB * m, 2 * SUB), 2 * SUB)
                for keep, at in ((False, 1 - core), (True, core)):
                    first = aligned(2 * SUB * m + SUB * at, SUB)
                    both = jnp.concatenate(
                        [res[pl.ds(first, SUB), :], res[pl.ds(aligned(CT + first, SUB), SUB), :]], axis=0
                    )
                    if keep:
                        mine[slot, h, rows] = both
                    else:
                        pair_out[k, h, rows] = both.astype(BF)

            pair(k, h).start()

    def send_rows(k):
        slot = lax.rem(k, 2)

        @pl.loop(0, 2)
        def _(h):
            pair(k, h).wait_recv()

            @pl.loop(0, CHIPS)
            def _(m):
                rows = pl.ds(aligned(2 * SUB * m, 2 * SUB), 2 * SUB)
                row_out[k, h, m] = (mine[slot, h, rows] + pair_in[k, h, rows].astype(F32)).astype(BF)

            for away in ALL:
                row_copy(k, h, away).start()

            row_in[k, h, chip] = row_out[k, h, chip]

    def finish(k):
        rows = pl.ds(aligned(SUB * k, SUB), SUB)
        for h in range(2):
            arrived(row_in.at[k, h, pl.ds(0, CHIPS - 1)], row_recv.at[k, h])

            total_k = row_in[k, h, 0].astype(F32)
            for m in range(1, CHIPS):
                total_k = total_k + row_in[k, h, m].astype(F32)
            cols = pl.ds(h * FH, FH)
            total[0, rows, cols] = total_k[:SUB]
            total[1, rows, cols] = total_k[SUB:]

    def d1(away):
        return remote(dbuf1.at[chip], dbuf1.at[chip], d1_recv.at[0], {"row": peer(away)[1]})

    quad = 2 * rep + core

    def d2(which):
        where = ({"row": sib}, {"rep": 1 - rep}, {"rep": 1 - rep, "row": sib})[which]
        return remote(dbuf2.at[quad], dbuf2.at[quad], d2_recv.at[0], where)

    @pl.loop(0, NCH + 3)
    def _(s):
        @pl.when(s < NCH)
        def _():
            work_terms(s)

        @pl.when(s == 0)
        def _():
            fold(2, NCH - 1)

        @pl.when(jnp.logical_and(s >= 2, s < NCH + 2))
        def _():
            send_rows(s - 2)

        @pl.when(jnp.logical_and(s >= 1, s < NCH + 1))
        def _():
            backward(s - 1)

        @pl.when(s < NCH)
        def _():
            forward_terms(s)

        @pl.when(s == NCH)
        def _():
            dbuf1[chip] = jnp.sum(dsum[...], axis=0, keepdims=True)
            for away in ALL:
                d1(away).start()

        @pl.when(s == NCH + 1)
        def _():
            arrived(dbuf1.at[pl.ds(0, CHIPS - 1)], d1_recv.at[0])
            dbuf2[quad] = jnp.sum(dbuf1[...], axis=0)
            for which in range(3):
                d2(which).start()

        @pl.when(s >= 3)
        def _():
            finish(s - 3)

    both_out[...] = total[...].astype(BF)
    arrived(dbuf2.at[pl.ds(0, 3)], d2_recv.at[0])
    diag_out[...] = jnp.sum(dbuf2[...], axis=0) * (1.0 / (REPS * ROWS * NCH * SUB))

    for block in (in0, in1, in2, red0, red1, red2, pair_out):
        sent(block)
    sent(gathered.at[pl.ds(0, CHIPS - 1)])
    sent(gathered.at[pl.ds(0, CHIPS)])
    sent(terms.at[:, :, pl.ds(0, 2 * OWN)])
    sent(terms.at[:, :, pl.ds(0, OWN)])
    sent(row_out.at[:, :, pl.ds(0, CHIPS - 1)])
    sent(dbuf1.at[pl.ds(0, CHIPS - 1)])
    sent(dbuf2.at[pl.ds(0, 3)])


def write_out(total, diag, grad_out, hess_out, diag_out):
    grad_out[...] = total[0]
    hess_out[...] = total[1]
    diag_out[...] = diag[...]


def local(tokens, probe_bits, cot_codes, cot_scales, w_gate, w_up, w_down):
    split = (ROWS, NCH, SUB)
    vm = pl.BlockSpec(memory_space=pltpu.VMEM)
    hbm = pl.BlockSpec(memory_space=pl.ANY)
    dma = pltpu.SemaphoreType.DMA
    total, diag = pl.pallas_call(
        kernel,
        out_shape=(
            jax.ShapeDtypeStruct((2, NCH * SUB, FE), BF),
            jax.ShapeDtypeStruct((1, FE), F32),
        ),
        in_specs=[hbm] * 7,
        out_specs=[vm] * 2,
        scratch_shapes=[
            pltpu.VMEM((FE, HI2), BF),
            pltpu.VMEM((HI, FE), BF),
            pltpu.VMEM((NCH, ROWS, SUB, FE), jnp.int32),
            pltpu.VMEM((NCH, ROWS, SUB, FE), jnp.int32),
            pltpu.VMEM((FE // 32, NCH * CT), jnp.int32),
            pltpu.VMEM((FE // 32, FE), BF),
            pltpu.VMEM((NCH * CT, FE // 32), BF),
            pltpu.VMEM((NCH, CT, FE), BF),
            pltpu.VMEM((2 * CT, FE), BF),
            pltpu.VMEM((ROWS, NCH * SUB, FE), BF),
            pltpu.VMEM((NCH, CT, FE), BF),
            pltpu.VMEM((NCH, CT, HI), BF),
            pltpu.VMEM((NCH, CT, HI2), BF),
            pltpu.VMEM((NCH, CT, HI2), BF),
            pltpu.VMEM((2, NCH, HALF, HI), BF),
            pltpu.VMEM((2, NCH, HALF, HI2), BF),
            pltpu.VMEM((2, NCH, HALF, HI2), BF),
            pltpu.VMEM((2, NCH, OWN, HI), BF),
            pltpu.VMEM((2, NCH, OWN, HI2), BF),
            pltpu.VMEM((2, NCH, OWN, HI2), BF),
            pltpu.VMEM((NCH, 2, CT, HI2), BF),
            pltpu.VMEM((2, NCH * SUB, FE), F32),
            pltpu.VMEM((2, 2, CT, FH), F32),
            pltpu.VMEM((NCH, 2, CT, FH), BF),
            pltpu.VMEM((NCH, 2, CT, FH), BF),
            pltpu.VMEM((NCH, 2, CHIPS, 2 * SUB, FH), BF),
            pltpu.VMEM((NCH, 2, CHIPS, 2 * SUB, FH), BF),
            pltpu.VMEM((8, FE), F32),
            pltpu.VMEM((CHIPS, 1, FE), F32),
            pltpu.VMEM((4, 1, FE), F32),
            pltpu.VMEM((2 * CT, FH), F32),
            dma((2 * NCH + 5,)), dma((1,)),
            dma((2,)), dma((1,)),
            dma((2 * NCH + 2,)), dma((2 * NCH + 2,)),
            dma((2, NCH)), dma((NCH,)),
            dma((NCH, 2)), dma((NCH, 2)),
            dma((1,)), dma((1,)),
            pltpu.SemaphoreType.REGULAR((2,)),
        ],
        compiler_params=pltpu.CompilerParams(
            collective_id=0, has_side_effects=True, vmem_limit_bytes=63 * 2**20
        ),
    )(
        tokens,
        probe_bits.reshape(split + (FE,)),
        cot_codes.reshape(split + (FE,)),
        cot_scales.T,
        w_gate,
        w_up,
        w_down,
    )
    return pl.pallas_call(
        write_out,
        out_shape=(
            jax.ShapeDtypeStruct((NCH * SUB, FE), BF),
            jax.ShapeDtypeStruct((NCH * SUB, FE), BF),
            jax.ShapeDtypeStruct((FE,), F32),
        ),
        in_specs=[vm] * 2,
        out_specs=[vm] * 3,
    )(total, diag.reshape(FE))


def solution(mesh):
    in_specs = (
        P(("rep", "row"), "col"),
        P("rep", "col"),
        P("rep", "col"),
        P("rep", "col"),
        P("col", "row"),
        P("col", "row"),
        P("row", "col"),
    )
    out_specs = (P(("rep", "row"), "col"), P(("rep", "row"), "col"), P("col"))
    return jax.shard_map(local, mesh=mesh, in_specs=in_specs, out_specs=out_specs, check_vma=False)
```
